256 devices in a mesh: tower: 2 (over z_hi), seq: 64 (over x, z_lo, y), rep: 2 (over core).
Axes of the slice: x: 4, y: 4, z: 8 (z_hi: 2, z_lo: 4; z = z_hi * 4 + z_lo), core: 2. Of those that a mesh axis runs over, the one named last changes fastest.
Arguments:
- query_rows: bfloat16 [2, 2, 16384, 1536], P('tower', 'rep', 'seq'), may hold values from -130 to 130
- key_rows: bfloat16 [2, 2, 16384, 1536], P('tower', 'rep', 'seq'), may hold values from -4 to 4
- value_rows: bfloat16 [2, 2, 16384, 1536], P('tower', 'rep', 'seq'), may hold values from -6 to 6
- out_grad: bfloat16 [2, 2, 16384, 1536], P('tower', 'rep', 'seq'), may hold values from -12 to 12
- query_gain: float32 [2, 1536], P('tower'), may hold values from 0.5 to 2
- live_counts: int32 [2, 64], replicated, may hold values from 128 to 256, as said below
- intersection: int32 [2, 64, 3], replicated, may hold values from 0 to 1, as said below
Outputs:
- attended: bfloat16 [2, 2, 16384, 1536], P('tower', 'rep', 'seq')
- query_grad: bfloat16 [2, 2, 16384, 1536], P('tower', 'rep', 'seq')
- key_grad: bfloat16 [2, 2, 16384, 1536], P('tower', 'rep', 'seq')
- value_grad: bfloat16 [2, 2, 16384, 1536], P('tower', 'rep', 'seq')
- gain_grad: float32 [2, 1536], P('tower')
The draws below stay inside these ranges and needn't reach their ends.
Inputs may be any that keep to these rules, and one draw needn't show every extreme that they name: `live_counts`: block 0 of each tower has 256 live tokens and block 1 has 128. `intersection`: every block intersections the other tower's block of the same index; the flags at offsets -1 and +1 vary.
All inputs are finite; a program needn't handle non-finite values.
Results may differ from the reference program's by a relative error of at most 0.0071.
Values may be sent and summed in bfloat16 or wider, within the bound.
A program may use at most 128 MiB of HBM per device.

```python
import math
import jax
import jax.numpy as jnp
from jax import lax

HEADS = 12
HEAD_DIM = 128
TOK = 256
BLOCKS = 64
CLIPS = 2
SEQLEN = 16384
WIDTH = 1536


def base_pair(key):
    shape = (2, CLIPS, BLOCKS * TOK, HEADS * HEAD_DIM)
    first = jnp.clip(jax.random.normal(jax.random.fold_in(key, 101), shape, jnp.float32), -4.0, 4.0)
    second = jnp.clip(jax.random.normal(jax.random.fold_in(key, 102), shape, jnp.float32), -4.0, 4.0)
    return (first, second)


def draw_query_rows(key, part):
    base_q, base_k = base_pair(key)
    return base_q.astype(jnp.bfloat16)


def draw_key_rows(key, part):
    base_q, base_k = base_pair(key)
    return base_k.astype(jnp.bfloat16)


def draw_out_grad(key, part):
    key = jax.random.fold_in(key, 5)
    shape = (2, CLIPS, BLOCKS * TOK, HEADS * HEAD_DIM)
    rising = 1.0 + 2.0 * jnp.arange(BLOCKS * TOK, dtype=jnp.float32) / (BLOCKS * TOK - 1)
    values = jnp.clip(jax.random.normal(key, shape, jnp.float32), -4.0, 4.0)
    return (values * rising[None, None, :, None]).astype(jnp.bfloat16)


def draw_live_counts(key, part):
    key = jax.random.fold_in(key, 6)
    counts = jax.random.randint(key, (2, BLOCKS), TOK // 2, TOK + 1, jnp.int32)
    counts = counts.at[:, 0].set(TOK)
    return counts.at[:, 1].set(TOK // 2)


def draw_intersection(key, part):
    key = jax.random.fold_in(key, 7)
    flags = jax.random.randint(key, (2, BLOCKS, 3), 0, 2, jnp.int32)
    return flags.at[:, :, 1].set(1)


def block_scale(key, dims, pieces, low, top_value):
    gain = 1.0
    for axis_at, blocks in pieces:
        heights = jax.random.uniform(jax.random.fold_in(jax.random.fold_in(key, 6), axis_at), (blocks,), jnp.float32, low / len(pieces), top_value / len(pieces))
        gain = gain * jnp.repeat(jnp.exp(heights), dims[axis_at] // blocks).reshape((-1,) + (1,) * (len(dims) - 1 - axis_at))
    return gain


def centred(stream_key, shape, scale, bound, cuts=(), kind=jnp.bfloat16):
    loudness = block_scale(stream_key, shape, cuts, -0.22, 0.18) if cuts else 1.0
    entries = jax.random.normal(stream_key, shape, jnp.float32) * scale * loudness
    return jnp.minimum(jnp.maximum(entries, -bound), bound).astype(kind)


def setup_inputs(seed: int = 0) -> dict:
    streams_of = jax.random.split(jax.random.key(seed), 8)
    return {
        "query_rows": draw_query_rows(jax.random.fold_in(streams_of[7], 71), 0),
        "key_rows": draw_key_rows(jax.random.fold_in(streams_of[7], 71), 0),
        "value_rows": centred(streams_of[2], (2, CLIPS, SEQLEN, WIDTH), 1.0, 6.0, ((0, 2), (1, 2), (2, 64))),
        "out_grad": draw_out_grad(jax.random.fold_in(streams_of[7], 71), 0),
        "query_gain": jnp.clip(jnp.exp(math.log(2.0) - 1.3862944 * jax.random.uniform(streams_of[4], (2, WIDTH), jnp.float32) ** block_scale(streams_of[4], (2, WIDTH), ((0, 2),), -0.2, 0.2)), 0.5, 2.0),
        "live_counts": draw_live_counts(jax.random.fold_in(streams_of[7], 71), 0),
        "intersection": draw_intersection(jax.random.fold_in(streams_of[7], 71), 0),
    }


def block_terms(query_block, key_wide, value_wide, grad_block, gain_row, key_live):
    width = HEADS * HEAD_DIM
    row_count = query_block.shape[0]
    score_scale = 1.0 / math.sqrt(HEAD_DIM)
    q_scaled = (query_block.astype(jnp.float32) * gain_row).astype(jnp.bfloat16)
    heads_q = q_scaled.astype(jnp.float32).reshape(row_count, HEADS, HEAD_DIM)
    heads_k = key_wide.astype(jnp.float32).reshape(3 * row_count, HEADS, HEAD_DIM)
    heads_v = value_wide.astype(jnp.float32).reshape(3 * row_count, HEADS, HEAD_DIM)
    heads_g = grad_block.astype(jnp.float32).reshape(row_count, HEADS, HEAD_DIM)
    scores = jnp.einsum('qhd,khd->hqk', heads_q, heads_k) * score_scale
    scores = jnp.where(key_live[None, None, :], scores, -1e+30)
    highest = lax.optimization_barrier(jnp.max(scores, axis=-1, keepdims=True))
    expo = jnp.exp(scores - highest)
    weights = expo / lax.optimization_barrier(jnp.sum(expo, axis=-1, keepdims=True))
    weights_low = weights.astype(jnp.bfloat16)
    attended = jnp.einsum('hqk,khd->qhd', weights_low.astype(jnp.float32), heads_v)
    attended = attended.reshape(row_count, width).astype(jnp.bfloat16)
    dprob = jnp.einsum('qhd,khd->hqk', heads_g, heads_v)
    center = lax.optimization_barrier(jnp.sum(weights * dprob, axis=-1, keepdims=True))
    dscore = (weights * (dprob - center) * score_scale).astype(jnp.bfloat16)
    dq_scaled = jnp.einsum('hqk,khd->qhd', dscore.astype(jnp.float32), heads_k).reshape(row_count, width)
    query_grad = (dq_scaled * gain_row).astype(jnp.bfloat16)
    gain_part = lax.optimization_barrier(jnp.sum(query_block.astype(jnp.float32) * dq_scaled, axis=0))
    key_part = jnp.einsum('hqk,qhd->khd', dscore.astype(jnp.float32), heads_q)
    key_part = key_part.reshape(3 * row_count, width).astype(jnp.bfloat16)
    value_part = jnp.einsum('hqk,qhd->khd', weights_low.astype(jnp.float32), heads_g)
    value_part = value_part.reshape(3 * row_count, width).astype(jnp.bfloat16)
    return (attended, query_grad, gain_part, key_part, value_part)

def gather_back(parts):
    width = HEADS * HEAD_DIM
    terms = parts.astype(jnp.float32).reshape(BLOCKS, 3, TOK, width)
    zero_block = jnp.zeros((1, TOK, width), jnp.float32)
    below = jnp.concatenate([zero_block, terms[:-1, 2]], axis=0)
    above = jnp.concatenate([terms[1:, 0], zero_block], axis=0)
    total = terms[:, 1] + below + above
    return total.astype(jnp.bfloat16).reshape(BLOCKS * TOK, width)

def reference(query_rows, key_rows, value_rows, out_grad, query_gain, live_counts, intersection):
    width = HEADS * HEAD_DIM
    attended_lists = [[], []]
    qgrad_lists = [[], []]
    kgrad_lists = [[None] * CLIPS, [None] * CLIPS]
    vgrad_lists = [[None] * CLIPS, [None] * CLIPS]
    gain_lists = []
    for tower_index in range(2):
        facing = 1 - tower_index
        gain_total = jnp.zeros((width,), jnp.float32)
        for clip_index in range(CLIPS):
            query_here = query_rows[tower_index, clip_index].reshape(BLOCKS, TOK, width)
            grad_here = out_grad[tower_index, clip_index].reshape(BLOCKS, TOK, width)
            padding = jnp.zeros((1, TOK, width), jnp.bfloat16)
            keys_padded = jnp.concatenate([padding, key_rows[facing, clip_index].reshape(BLOCKS, TOK, width), padding], axis=0)
            values_padded = jnp.concatenate([padding, value_rows[facing, clip_index].reshape(BLOCKS, TOK, width), padding], axis=0)
            gain_row = query_gain[tower_index]

            def one_block(block_index):
                key_wide = lax.dynamic_slice_in_dim(keys_padded, block_index, 3, 0).reshape(3 * TOK, width)
                value_wide = lax.dynamic_slice_in_dim(values_padded, block_index, 3, 0).reshape(3 * TOK, width)
                query_block = lax.dynamic_index_in_dim(query_here, block_index, 0, False)
                grad_block = lax.dynamic_index_in_dim(grad_here, block_index, 0, False)
                neighbour = block_index - 1 + jnp.arange(3, dtype=jnp.int32)
                present = (neighbour >= 0) & (neighbour < BLOCKS)
                counts_near = jnp.take(live_counts[facing], jnp.clip(neighbour, 0, BLOCKS - 1))
                flags = lax.dynamic_index_in_dim(intersection[tower_index], block_index, 0, False)
                position = jnp.arange(TOK, dtype=jnp.int32)
                key_live = present[:, None] & (flags[:, None] == 1) & (position[None, :] < counts_near[:, None])
                return block_terms(query_block, key_wide, value_wide, grad_block, gain_row, key_live.reshape(3 * TOK))
            results = lax.map(one_block, jnp.arange(BLOCKS, dtype=jnp.int32))
            attended_part, qgrad_part, gain_part, key_part, value_part = results
            attended_lists[tower_index].append(attended_part.reshape(BLOCKS * TOK, width))
            qgrad_lists[tower_index].append(qgrad_part.reshape(BLOCKS * TOK, width))
            kgrad_lists[facing][clip_index] = gather_back(key_part)
            vgrad_lists[facing][clip_index] = gather_back(value_part)
            gain_total = gain_total + lax.optimization_barrier(jnp.sum(gain_part, axis=0))
        gain_lists.append(gain_total)
    attended = jnp.stack([jnp.stack(attended_lists[0]), jnp.stack(attended_lists[1])])
    query_grad = jnp.stack([jnp.stack(qgrad_lists[0]), jnp.stack(qgrad_lists[1])])
    key_grad = jnp.stack([jnp.stack(kgrad_lists[0]), jnp.stack(kgrad_lists[1])])
    value_grad = jnp.stack([jnp.stack(vgrad_lists[0]), jnp.stack(vgrad_lists[1])])
    gain_grad = jnp.stack(gain_lists)
    return (attended, query_grad, key_grad, value_grad, gain_grad)
```

```python
import functools
import math

import jax
import jax.numpy as jnp
from jax import lax
from jax.experimental import pallas as pl
from jax.experimental.pallas import tpu as pltpu
from jax.sharding import PartitionSpec as P

HEADS = 12
DIM = 128
TOK = 256
BLOCKS = 64
WIDE = 3 * TOK
WIDTH = HEADS * DIM
SCALE = 1.0 / math.sqrt(DIM)
MESH = pl.DeviceIdType.MESH
BF = jnp.bfloat16
F32 = jnp.float32


def dot(a, b, ca, cb):
    return lax.dot_general(a, b, (((ca,), (cb,)), ((), ())), preferred_element_type=F32)


def kernel(
    q_hbm, k_hbm, v_hbm, g_hbm, gain_ref, counts_ref, flags_ref,
    att_hbm, dq_hbm, dk_hbm, dv_hbm, gg_ref,
    q_buf, g_buf, wide, term_out, term_in, term_mid, total, att_buf, dq_buf, gsum, gred,
    load_sem, swap_send, swap_recv, fwd_send, fwd_recv, term_send, term_recv,
    fin_send, fin_recv, store_sem, gain_send, gain_recv,
):
    tower = lax.axis_index("tower")
    seq = lax.axis_index("seq")
    rep = lax.axis_index("rep")
    x_at, z_at, y_at = seq // 16, (seq // 4) % 4, seq % 4

    partner = (1 - tower, seq, rep)
    below = (tower, lax.rem(seq + BLOCKS - 1, BLOCKS), rep)
    above = (tower, lax.rem(seq + 1, BLOCKS), rep)

    def along(axis, step):
        if axis == 0:
            return (tower, seq, 1 - rep)
        if axis == 1:
            return (tower, x_at * 16 + z_at * 4 + (y_at + step) % 4, rep)
        if axis == 2:
            return (tower, ((x_at + step) % 4) * 16 + z_at * 4 + y_at, rep)
        return (tower, x_at * 16 + ((z_at + step) % 4) * 4 + y_at, rep)

    group = (2, 4, 4, 4)
    place = (rep, y_at, x_at, z_at)

    loads = [
        pltpu.make_async_copy(q_hbm, q_buf, load_sem.at[0]),
        pltpu.make_async_copy(g_hbm, g_buf, load_sem.at[1]),
    ]
    for copy in loads:
        copy.start()

    barrier = pltpu.get_barrier_semaphore()
    greeted = [partner, below, above]
    for axis in range(4):
        greeted += [along(axis, step) for step in range(1, group[axis])]
    for device in greeted:
        pl.semaphore_signal(barrier, inc=1, device_id=device, device_id_type=MESH)
    pl.semaphore_wait(barrier, len(greeted))

    def columns(h):
        return pl.ds(pl.multiple_of(h * DIM, DIM), DIM)

    def swap_copies(h):
        return [
            pltpu.make_async_remote_copy(
                src_ref=src.at[:, columns(h)],
                dst_ref=wide.at[h, i, pl.ds(TOK, TOK)],
                send_sem=swap_send.at[h, i],
                recv_sem=swap_recv.at[h, i],
                device_id=partner,
                device_id_type=MESH,
            )
            for i, src in ((0, k_hbm), (1, v_hbm))
        ]

    def forward_copies(h):
        return [
            pltpu.make_async_remote_copy(
                src_ref=wide.at[h, :, pl.ds(TOK, TOK)],
                dst_ref=wide.at[h, :, pl.ds(0 if i == 0 else 2 * TOK, TOK)],
                send_sem=fwd_send.at[h, i],
                recv_sem=fwd_recv.at[h, i],
                device_id=device,
                device_id_type=MESH,
            )
            for i, device in ((0, above), (1, below))
        ]

    def term_copies(h):
        return [
            pltpu.make_async_remote_copy(
                src_ref=term_out.at[h, i],
                dst_ref=term_in.at[h, i],
                send_sem=term_send.at[h, i],
                recv_sem=term_recv.at[h, i],
                device_id=device,
                device_id_type=MESH,
            )
            for i, device in ((0, below), (1, above))
        ]

    def final_copies(h):
        return [
            pltpu.make_async_remote_copy(
                src_ref=total.at[h, i],
                dst_ref=dst.at[:, columns(h)],
                send_sem=fin_send.at[h, i],
                recv_sem=fin_recv.at[h, i],
                device_id=partner,
                device_id_type=MESH,
            )
            for i, dst in ((0, dk_hbm), (1, dv_hbm))
        ]

    def store_copies(h):
        return [
            pltpu.make_async_copy(att_buf.at[h], att_hbm.at[:, columns(h)], store_sem.at[h, 0]),
            pltpu.make_async_copy(dq_buf.at[h], dq_hbm.at[:, columns(h)], store_sem.at[h, 1]),
        ]

    @pl.loop(0, HEADS)
    def _(h):
        for copy in swap_copies(h):
            copy.start()

    position = lax.broadcasted_iota(jnp.int32, (1, TOK), 1)
    bias = []
    for j in range(3):
        near = seq + (j - 1)
        inside = jnp.clip(near, 0, BLOCKS - 1)
        open_ = (near == inside) & (flags_ref[tower, seq * 3 + j] == 1)
        live = jnp.where(open_, counts_ref[1 - tower, inside], 0)
        bias.append(jnp.where(position < live, 0.0, -1e30).astype(F32))
    bias = jnp.concatenate(bias, axis=1)
    gsum[...] = jnp.zeros_like(gsum)

    for copy in loads:
        copy.wait()

    def forward(h):
        for copy in swap_copies(h):
            copy.wait_recv()
        for copy in forward_copies(h):
            copy.start()

    def compute(h):
        for copy in forward_copies(h):
            copy.wait_recv()
        gain = gain_ref[:, columns(h)]
        q_raw = q_buf[:, columns(h)].astype(F32)
        q = (q_raw * gain).astype(BF)
        g = g_buf[:, columns(h)]
        keys = wide[h, 0]
        values = wide[h, 1]
        scores = dot(q, keys, 1, 1) * SCALE + bias
        highest = jnp.max(scores, axis=1, keepdims=True)
        expo = jnp.exp(scores - highest)
        probs = expo / jnp.sum(expo, axis=1, keepdims=True)
        low = probs.astype(BF)
        att_buf[h] = dot(low, values, 1, 0).astype(BF)
        dprob = dot(g, values, 1, 1)
        center = jnp.sum(probs * dprob, axis=1, keepdims=True)
        dscore = (probs * (dprob - center) * SCALE).astype(BF)
        dscaled = dot(dscore, keys, 1, 0)
        dq_buf[h] = (dscaled * gain).astype(BF)
        gsum[pl.ds(h, 1), :] = jnp.sum(q_raw * dscaled, axis=0, keepdims=True)
        for i, (left, right) in enumerate(((dscore, q), (low, g))):
            terms = dot(left, right, 0, 0).astype(BF)
            term_out[h, 0, i] = terms[:TOK]
            term_mid[h, i] = terms[TOK : 2 * TOK]
            term_out[h, 1, i] = terms[2 * TOK :]
        for copy in term_copies(h):
            copy.start()
        for copy in store_copies(h):
            copy.start()

    def finish(h):
        for copy in term_copies(h):
            copy.wait_recv()
        for i in range(2):
            total[h, i] = (
                term_mid[h, i].astype(F32)
                + term_in[h, 0, i].astype(F32)
                + term_in[h, 1, i].astype(F32)
            ).astype(BF)
        for copy in final_copies(h):
            copy.start()

    @pl.loop(0, HEADS + 2)
    def _(step):
        @pl.when(step < HEADS)
        def _():
            forward(step)

        @pl.when((step >= 1) & (step < HEADS + 1))
        def _():
            compute(step - 1)

        @pl.when(step >= 2)
        def _():
            finish(step - 2)

    def gain_copies(axis):
        return [
            pltpu.make_async_remote_copy(
                src_ref=gred.at[axis, place[axis]],
                dst_ref=gred.at[axis, place[axis]],
                send_sem=gain_send.at[axis, step],
                recv_sem=gain_recv.at[axis, step],
                device_id=along(axis, step),
                device_id_type=MESH,
            )
            for step in range(1, group[axis])
        ]

    def gain_arrivals(axis):
        return [
            pltpu.make_async_remote_copy(
                src_ref=gred.at[axis, 0],
                dst_ref=gred.at[axis, (place[axis] + group[axis] - step) % group[axis]],
                send_sem=gain_send.at[axis, step],
                recv_sem=gain_recv.at[axis, step],
                device_id=along(axis, step),
                device_id_type=MESH,
            )
            for step in range(1, group[axis])
        ]

    part = gsum[...]
    for axis in range(4):
        gred[axis, place[axis]] = part
        for copy in gain_copies(axis):
            copy.start()
        for copy in gain_arrivals(axis):
            copy.wait_recv()
        for copy in gain_copies(axis):
            copy.wait_send()
        part = gred[axis, 0]
        for slot in range(1, group[axis]):
            part = part + gred[axis, slot]
    gg_ref[...] = part[:HEADS]

    @pl.loop(0, HEADS)
    def _(h):
        for copy in swap_copies(h) + forward_copies(h) + term_copies(h) + final_copies(h):
            copy.wait_send()
        for copy in store_copies(h):
            copy.wait()

    @pl.loop(0, HEADS)
    def _(h):
        for copy in final_copies(h):
            copy.wait_recv()


def per_device(query_rows, key_rows, value_rows, out_grad, query_gain, live_counts, intersection):
    flags = intersection.reshape(2, BLOCKS * 3)
    anywhere = pl.BlockSpec(memory_space=pl.ANY)
    vmem = pl.BlockSpec(memory_space=pltpu.VMEM)
    smem = pl.BlockSpec(memory_space=pltpu.SMEM)
    block = jax.ShapeDtypeStruct((TOK, WIDTH), BF)
    dma = pltpu.SemaphoreType.DMA
    pair = (HEADS, 2)
    results = pl.pallas_call(
        kernel,
        out_shape=(block, block, block, block, jax.ShapeDtypeStruct((HEADS, DIM), F32)),
        in_specs=[anywhere] * 4 + [vmem, smem, smem],
        out_specs=(anywhere,) * 4 + (vmem,),
        scratch_shapes=[
            pltpu.VMEM((TOK, WIDTH), BF),
            pltpu.VMEM((TOK, WIDTH), BF),
            pltpu.VMEM((HEADS, 2, WIDE, DIM), BF),
            pltpu.VMEM((HEADS, 2, 2, TOK, DIM), BF),
            pltpu.VMEM((HEADS, 2, 2, TOK, DIM), BF),
            pltpu.VMEM((HEADS, 2, TOK, DIM), BF),
            pltpu.VMEM((HEADS, 2, TOK, DIM), BF),
            pltpu.VMEM((HEADS, TOK, DIM), BF),
            pltpu.VMEM((HEADS, TOK, DIM), BF),
            pltpu.VMEM((16, DIM), F32),
            pltpu.VMEM((4, 4, 16, DIM), F32),
            dma((2,)), dma(pair), dma(pair), dma(pair), dma(pair), dma(pair), dma(pair),
            dma(pair), dma(pair), dma(pair), dma((4, 4)), dma((4, 4)),
        ],
        compiler_params=pltpu.CompilerParams(
            collective_id=0, has_side_effects=True, vmem_limit_bytes=48 * 2**20
        ),
        name="cross_attention",
    )(
        query_rows[0, 0], key_rows[0, 0], value_rows[0, 0], out_grad[0, 0],
        query_gain, live_counts, flags,
    )
    shape = (1, 1, TOK, WIDTH)
    return tuple(r.reshape(shape) for r in results[:4]) + (results[4].reshape(1, WIDTH),)


def solution(mesh):
    rows = P("tower", "rep", "seq", None)
    return jax.shard_map(
        per_device,
        mesh=mesh,
        in_specs=(rows, rows, rows, rows, P("tower", None), P(), P()),
        out_specs=(rows, rows, rows, rows, P("tower", None)),
        check_vma=False,
    )
```

```python
import functools
import math

import jax
import jax.numpy as jnp
from jax import lax
from jax.experimental import pallas as pl
from jax.experimental.pallas import tpu as pltpu
from jax.sharding import PartitionSpec as P

HEADS = 12
DIM = 128
TOK = 256
BLOCKS = 64
WIDE = 3 * TOK
WIDTH = HEADS * DIM
SCALE = 1.0 / math.sqrt(DIM)
AHEAD = 1
VMEM_MIB = 60
MESH = pl.DeviceIdType.MESH
BF = jnp.bfloat16
F32 = jnp.float32


def dot(a, b, ca, cb):
    return lax.dot_general(a, b, (((ca,), (cb,)), ((), ())), preferred_element_type=F32)


def kernel(
    q_hbm, k_hbm, v_hbm, g_hbm, gain_ref, counts_ref, flags_ref,
    att_hbm, dq_hbm, dk_hbm, dv_hbm, gg_ref,
    q_buf, g_buf, wide, rel_in, term_out, term_in, term_mid, total,
    part_in, cross_in, rel_total, att_buf, dq_buf, gsum, gred,
    load_sem, swap_send, rel_recv, relay_send, kv_recv, fwd_send,
    term_send, term_recv, part_send, part_recv, cross_recv,
    fin_send, fin_recv, store_sem, gain_send, gain_recv,
):
    tower = lax.axis_index("tower")
    seq = lax.axis_index("seq")
    rep = lax.axis_index("rep")
    x_at, z_at, y_at = seq // 16, (seq // 4) % 4, seq % 4

    first = y_at == 0
    outer = first | (y_at == 3)
    inner = jnp.logical_not(outer)
    side = jnp.where(first, 3, 1)
    toward = jnp.where(first, BLOCKS - 1, 1)
    fwd_slot = jnp.where(first, 0, 2)
    cross_slot = 2 - fwd_slot
    cross_side = jnp.where(first, 0, 1)
    in_side = 1 - cross_side

    def shifted(block, step):
        return (block + step) % BLOCKS

    def along_z(block, step):
        return (block // 16) * 16 + ((block // 4 + step) % 4) * 4 + block % 4

    partner = (1 - tower, seq, rep)
    below = (tower, shifted(seq, BLOCKS - 1), rep)
    above = (tower, shifted(seq, 1), rep)
    my_relay = along_z(seq, side)
    relayed = along_z(seq, 4 - side)
    far_relay = (1 - tower, my_relay, rep)
    near_relay = (tower, my_relay, rep)
    relayed_home = (1 - tower, relayed, rep)
    relayed_query = (tower, relayed, rep)
    relayed_next = (tower, shifted(relayed, toward), rep)
    inside_next = (tower, shifted(seq, BLOCKS - toward), rep)
    term_relay = (tower, along_z(shifted(seq, toward), 4 - side), rep)

    def along(axis, step):
        if axis == 0:
            return (tower, seq, 1 - rep)
        if axis == 1:
            return (tower, x_at * 16 + z_at * 4 + (y_at + step) % 4, rep)
        if axis == 2:
            return (tower, ((x_at + step) % 4) * 16 + z_at * 4 + y_at, rep)
        return (tower, along_z(seq, step), rep)

    group = (2, 4, 4, 4)
    place = (rep, y_at, x_at, z_at)

    loads = [
        pltpu.make_async_copy(q_hbm, q_buf, load_sem.at[0]),
        pltpu.make_async_copy(g_hbm, g_buf, load_sem.at[1]),
    ]
    for copy in loads:
        copy.start()

    barrier = pltpu.get_barrier_semaphore()

    def greet(devices):
        for device in devices:
            pl.semaphore_signal(barrier, inc=1, device_id=device, device_id_type=MESH)
        pl.semaphore_wait(barrier, len(devices))

    everyone = []
    for axis in range(4):
        everyone += [along(axis, step) for step in range(1, group[axis])]

    @pl.when(inner)
    def _():
        greet(everyone + [partner, below, above])

    @pl.when(outer)
    def _():
        greet(
            everyone
            + [inside_next, far_relay, near_relay, relayed_home]
            + [relayed_query, relayed_next, term_relay]
        )

    def columns(h):
        return pl.ds(pl.multiple_of(h * DIM, DIM), DIM)

    def remote(src, dst, send, recv, device):
        return pltpu.make_async_remote_copy(
            src_ref=src,
            dst_ref=dst,
            send_sem=send,
            recv_sem=recv,
            device_id=device,
            device_id_type=MESH,
        )

    sources = ((0, k_hbm), (1, v_hbm))
    targets = ((0, dk_hbm), (1, dv_hbm))

    def swap_copies(h):
        return [
            remote(
                src.at[:, columns(h)], wide.at[h, 1, i],
                swap_send.at[h, i], kv_recv.at[h, 1 + 2 * i], partner,
            )
            for i, src in sources
        ]

    def first_copies(h):
        return [
            remote(
                src.at[:, columns(h)], rel_in.at[h, i],
                swap_send.at[h, i], rel_recv.at[h, i], far_relay,
            )
            for i, src in sources
        ]

    def relay_copies(h):
        return [
            remote(
                rel_in.at[h], wide.at[h, 1],
                relay_send.at[h, 0], kv_recv.at[h, 1], relayed_query,
            ),
            remote(
                rel_in.at[h], wide.at[h, cross_slot],
                relay_send.at[h, 1], kv_recv.at[h, cross_slot], relayed_next,
            ),
        ]

    def forward_inner(h):
        return [
            remote(wide.at[h, 1], wide.at[h, 2], fwd_send.at[h, 0], kv_recv.at[h, 2], below),
            remote(wide.at[h, 1], wide.at[h, 0], fwd_send.at[h, 1], kv_recv.at[h, 0], above),
        ]

    def forward_outer(h):
        return [
            remote(
                wide.at[h, 1], wide.at[h, fwd_slot],
                fwd_send.at[h, 0], kv_recv.at[h, fwd_slot], inside_next,
            )
        ]

    def near_arrivals(h):
        return [
            remote(wide.at[h, 1], wide.at[h, j], fwd_send.at[h, 0], kv_recv.at[h, j], above)
            for j in (0, 2)
        ]

    def terms_inner(h):
        return [
            remote(
                term_out.at[h, i], term_in.at[h, i],
                term_send.at[h, i], term_recv.at[h, i], device,
            )
            for i, device in ((0, below), (1, above))
        ]

    def terms_outer(h):
        return [
            remote(
                term_out.at[h, in_side], term_in.at[h, in_side],
                term_send.at[h, 0], term_recv.at[h, in_side], inside_next,
            ),
            remote(
                term_out.at[h, cross_side], cross_in.at[h],
                term_send.at[h, 1], cross_recv.at[h], term_relay,
            ),
        ]

    def term_arrival(h):
        return remote(
            term_out.at[h, 0], term_in.at[h, cross_side],
            term_send.at[h, 0], term_recv.at[h, cross_side], inside_next,
        )

    def part_copy(h):
        return remote(
            total.at[h], part_in.at[h], part_send.at[h], part_recv.at[h], near_relay
        )

    def final_copies(h, src, device):
        return [
            remote(
                src.at[h, i], dst.at[:, columns(h)], fin_send.at[h, i], fin_recv.at[h, i], device
            )
            for i, dst in targets
        ]

    def store_copies(h):
        return [
            pltpu.make_async_copy(att_buf.at[h], att_hbm.at[:, columns(h)], store_sem.at[h, 0]),
            pltpu.make_async_copy(dq_buf.at[h], dq_hbm.at[:, columns(h)], store_sem.at[h, 1]),
        ]

    def begin(copies):
        for copy in copies:
            copy.start()

    def arrived(copies):
        for copy in copies:
            copy.wait_recv()

    def sent(copies):
        for copy in copies:
            copy.wait_send()

    def send_home(h):
        @pl.when(inner)
        def _():
            begin(swap_copies(h))

        @pl.when(outer)
        def _():
            begin(first_copies(h))

    @pl.loop(0, AHEAD)
    def _(h):
        send_home(h)

    position = lax.broadcasted_iota(jnp.int32, (1, TOK), 1)
    bias = []
    for j in range(3):
        neighbour = seq + (j - 1)
        inside = jnp.clip(neighbour, 0, BLOCKS - 1)
        open_ = (neighbour == inside) & (flags_ref[tower, seq, j] == 1)
        live = jnp.where(open_, counts_ref[1 - tower, inside], 0)
        bias.append(jnp.where(position < live, 0.0, -1e30).astype(F32))
    bias = jnp.concatenate(bias, axis=1)
    gsum[...] = jnp.zeros_like(gsum)

    for copy in loads:
        copy.wait()

    def relay(h):
        @pl.when(outer)
        def _():
            arrived(first_copies(h))
            begin(relay_copies(h))

    def forward(h):
        @pl.when(outer)
        def _():
            arrived(relay_copies(h)[:1])
            begin(forward_outer(h))

        @pl.when(inner)
        def _():
            arrived(swap_copies(h))
            begin(forward_inner(h))

    def compute(h):
        arrived(near_arrivals(h))
        gain = gain_ref[:, columns(h)]
        q_raw = q_buf[:, columns(h)].astype(F32)
        q = (q_raw * gain).astype(BF)
        g = g_buf[:, columns(h)]
        keys = wide[h, :, 0].reshape(WIDE, DIM)
        values = wide[h, :, 1].reshape(WIDE, DIM)
        scores = dot(q, keys, 1, 1) * SCALE + bias
        highest = jnp.max(scores, axis=1, keepdims=True)
        expo = jnp.exp(scores - highest)
        probs = expo / jnp.sum(expo, axis=1, keepdims=True)
        low = probs.astype(BF)
        att_buf[h] = dot(low, values, 1, 0).astype(BF)
        dprob = dot(g, values, 1, 1)
        center = jnp.sum(probs * dprob, axis=1, keepdims=True)
        dscore = (probs * (dprob - center) * SCALE).astype(BF)
        dscaled = dot(dscore, keys, 1, 0)
        dq_buf[h] = (dscaled * gain).astype(BF)
        gsum[pl.ds(h, 1), :] = jnp.sum(q_raw * dscaled, axis=0, keepdims=True)
        for i, (left, right) in enumerate(((dscore, q), (low, g))):
            terms = dot(left, right, 0, 0).astype(BF)
            term_out[h, 0, i] = terms[:TOK]
            term_mid[h, i] = terms[TOK : 2 * TOK]
            term_out[h, 1, i] = terms[2 * TOK :]

        @pl.when(inner)
        def _():
            begin(terms_inner(h))

        @pl.when(outer)
        def _():
            begin(terms_outer(h))

        begin(store_copies(h))

    def gather(h):
        @pl.when(inner)
        def _():
            arrived(terms_inner(h))
            for i in range(2):
                total[h, i] = (
                    term_mid[h, i].astype(F32)
                    + term_in[h, 0, i].astype(F32)
                    + term_in[h, 1, i].astype(F32)
                ).astype(BF)
            begin(final_copies(h, total, partner))

        @pl.when(outer)
        def _():
            term_arrival(h).wait_recv()
            total[h] = (
                term_mid[h].astype(F32) + term_in[h, cross_side].astype(F32)
            ).astype(BF)
            part_copy(h).start()

    def pass_on(h):
        @pl.when(outer)
        def _():
            part_copy(h).wait_recv()
            terms_outer(h)[1].wait_recv()
            rel_total[h] = (part_in[h].astype(F32) + cross_in[h].astype(F32)).astype(BF)
            begin(final_copies(h, rel_total, relayed_home))

    @pl.loop(0, HEADS + 2)
    def _(step):
        @pl.when(step < HEADS - AHEAD)
        def _():
            send_home(step + AHEAD)

        @pl.when(step < HEADS)
        def _():
            relay(step)

        @pl.when((step >= 1) & (step < HEADS + 1))
        def _():
            forward(step - 1)

        @pl.when(step >= 2)
        def _():
            compute(step - 2)

        @pl.when(step >= 3)
        def _():
            gather(step - 3)

        @pl.when(step >= 4)
        def _():
            pass_on(step - 4)

    def gain_copies(axis):
        return [
            remote(
                gred.at[axis, place[axis]], gred.at[axis, place[axis]],
                gain_send.at[axis, step], gain_recv.at[axis, step], along(axis, step),
            )
            for step in range(1, group[axis])
        ]

    def gain_arrivals(axis):
        return [
            remote(
                gred.at[axis, 0],
                gred.at[axis, (place[axis] + group[axis] - step) % group[axis]],
                gain_send.at[axis, step], gain_recv.at[axis, step], along(axis, step),
            )
            for step in range(1, group[axis])
        ]

    def gain_begin(axis, part):
        gred[axis, place[axis]] = part
        begin(gain_copies(axis))

    def gain_end(axis):
        arrived(gain_arrivals(axis))
        part = gred[axis, 0]
        for slot in range(1, group[axis]):
            part = part + gred[axis, slot]
        return part

    gain_begin(0, gsum[...])
    gather(HEADS - 1)
    gain_begin(1, gain_end(0))
    pass_on(HEADS - 2)
    gain_begin(2, gain_end(1))
    pass_on(HEADS - 1)
    gain_begin(3, gain_end(2))
    gg_ref[...] = gain_end(3)[:HEADS]
    for axis in range(4):
        sent(gain_copies(axis))

    @pl.loop(0, HEADS)
    def _(h):
        @pl.when(inner)
        def _():
            sent(swap_copies(h) + forward_inner(h) + terms_inner(h))

        @pl.when(outer)
        def _():
            sent(first_copies(h) + relay_copies(h) + forward_outer(h) + terms_outer(h))
            sent([part_copy(h)])

        sent(final_copies(h, total, partner))
        for copy in store_copies(h):
            copy.wait()

    @pl.loop(0, HEADS)
    def _(h):
        arrived(final_copies(h, total, partner))


def per_device(query_rows, key_rows, value_rows, out_grad, query_gain, live_counts, intersection):
    anywhere = pl.BlockSpec(memory_space=pl.ANY)
    vmem = pl.BlockSpec(memory_space=pltpu.VMEM)
    smem = pl.BlockSpec(memory_space=pltpu.SMEM)
    block = jax.ShapeDtypeStruct((TOK, WIDTH), BF)
    dma = pltpu.SemaphoreType.DMA
    pair = (HEADS, 2)
    results = pl.pallas_call(
        kernel,
        out_shape=(block, block, block, block, jax.ShapeDtypeStruct((HEADS, DIM), F32)),
        in_specs=[anywhere] * 4 + [vmem, smem, smem],
        out_specs=(anywhere,) * 4 + (vmem,),
        scratch_shapes=[
            pltpu.VMEM((TOK, WIDTH), BF),
            pltpu.VMEM((TOK, WIDTH), BF),
            pltpu.VMEM((HEADS, 3, 2, TOK, DIM), BF),
            pltpu.VMEM((HEADS, 2, TOK, DIM), BF),
            pltpu.VMEM((HEADS, 2, 2, TOK, DIM), BF),
            pltpu.VMEM((HEADS, 2, 2, TOK, DIM), BF),
            pltpu.VMEM((HEADS, 2, TOK, DIM), BF),
            pltpu.VMEM((HEADS, 2, TOK, DIM), BF),
            pltpu.VMEM((HEADS, 2, TOK, DIM), BF),
            pltpu.VMEM((HEADS, 2, TOK, DIM), BF),
            pltpu.VMEM((HEADS, 2, TOK, DIM), BF),
            pltpu.VMEM((HEADS, TOK, DIM), BF),
            pltpu.VMEM((HEADS, TOK, DIM), BF),
            pltpu.VMEM((16, DIM), F32),
            pltpu.VMEM((4, 4, 16, DIM), F32),
            dma((2,)), dma(pair), dma(pair), dma(pair), dma((HEADS, 4)), dma(pair),
            dma(pair), dma(pair), dma((HEADS,)), dma((HEADS,)), dma((HEADS,)),
            dma(pair), dma(pair), dma(pair), dma((4, 4)), dma((4, 4)),
        ],
        compiler_params=pltpu.CompilerParams(
            collective_id=0, has_side_effects=True, vmem_limit_bytes=VMEM_MIB * 2**20
        ),
        name="cross_attention",
    )(
        query_rows[0, 0], key_rows[0, 0], value_rows[0, 0], out_grad[0, 0],
        query_gain, live_counts, intersection,
    )
    shape = (1, 1, TOK, WIDTH)
    return tuple(r.reshape(shape) for r in results[:4]) + (results[4].reshape(1, WIDTH),)


def solution(mesh):
    rows = P("tower", "rep", "seq", None)
    return jax.shard_map(
        per_device,
        mesh=mesh,
        in_specs=(rows, rows, rows, rows, P("tower", None), P(), P()),
        out_specs=(rows, rows, rows, rows, P("tower", None)),
        check_vma=False,
    )
```

```python
import functools
import math

import jax
import jax.numpy as jnp
from jax import lax
from jax.experimental import pallas as pl
from jax.experimental.pallas import tpu as pltpu
from jax.sharding import PartitionSpec as P

HEADS = 12
DIM = 128
TOK = 256
BLOCKS = 64
WIDE = 3 * TOK
WIDTH = HEADS * DIM
SCALE = 1.0 / math.sqrt(DIM)
PARTS = 2 * HEADS
AHEAD = 1
LAGS = (0, 1, 2, 3, 4)
VMEM_MIB = 60
MESH = pl.DeviceIdType.MESH
BF = jnp.bfloat16
F32 = jnp.float32


def dot(a, b, ca, cb):
    return lax.dot_general(a, b, (((ca,), (cb,)), ((), ())), preferred_element_type=F32)


def kernel(
    q_hbm, k_hbm, v_hbm, g_hbm, gain_hbm, counts_hbm, flags_hbm,
    att_hbm, dq_hbm, dk_hbm, dv_hbm, gg_ref,
    q_buf, g_buf, gain_ref, counts_ref, flags_ref, wide, rel_in, term_out, term_in, term_mid, total,
    part_in, cross_in, rel_total, probs_buf, low_buf, q_scaled, att_buf, dq_buf, gsum, gred,
    load_sem, swap_send, rel_recv, relay_send, kv_recv, fwd_send,
    term_send, term_recv, part_send, part_recv, cross_recv,
    fin_send, fin_recv, store_sem, gain_send, gain_recv,
):
    tower = lax.axis_index("tower")
    seq = lax.axis_index("seq")
    rep = lax.axis_index("rep")
    x_at, z_at, y_at = seq // 16, (seq // 4) % 4, seq % 4

    first = y_at == 0
    outer = first | (y_at == 3)
    inner = jnp.logical_not(outer)
    side = jnp.where(first, 3, 1)
    toward = jnp.where(first, BLOCKS - 1, 1)
    fwd_slot = jnp.where(first, 0, 2)
    cross_slot = 2 - fwd_slot
    cross_side = jnp.where(first, 0, 1)
    in_side = 1 - cross_side

    def shifted(block, step):
        return (block + step) % BLOCKS

    def along_z(block, step):
        return (block // 16) * 16 + ((block // 4 + step) % 4) * 4 + block % 4

    partner = (1 - tower, seq, rep)
    below = (tower, shifted(seq, BLOCKS - 1), rep)
    above = (tower, shifted(seq, 1), rep)
    my_relay = along_z(seq, side)
    relayed = along_z(seq, 4 - side)
    far_relay = (1 - tower, my_relay, rep)
    near_relay = (tower, my_relay, rep)
    relayed_home = (1 - tower, relayed, rep)
    relayed_query = (tower, relayed, rep)
    relayed_next = (tower, shifted(relayed, toward), rep)
    inside_next = (tower, shifted(seq, BLOCKS - toward), rep)
    term_relay = (tower, along_z(shifted(seq, toward), 4 - side), rep)

    group = (8, 4, 4)
    place = (y_at * 2 + rep, x_at, z_at)

    def along(axis, step):
        if axis == 0:
            spot = (place[0] + step) % 8
            return (tower, x_at * 16 + z_at * 4 + spot // 2, spot % 2)
        if axis == 1:
            return (tower, ((x_at + step) % 4) * 16 + z_at * 4 + y_at, rep)
        return (tower, along_z(seq, step), rep)

    loads = [
        pltpu.make_async_copy(q_hbm, q_buf, load_sem.at[0]),
        pltpu.make_async_copy(g_hbm, g_buf, load_sem.at[1]),
        pltpu.make_async_copy(gain_hbm, gain_ref, load_sem.at[2]),
        pltpu.make_async_copy(counts_hbm, counts_ref, load_sem.at[3]),
        pltpu.make_async_copy(flags_hbm, flags_ref, load_sem.at[4]),
    ]
    for copy in loads:
        copy.start()

    barrier = pltpu.get_barrier_semaphore()

    def greet(devices):
        for device in devices:
            pl.semaphore_signal(barrier, inc=1, device_id=device, device_id_type=MESH)
        pl.semaphore_wait(barrier, len(devices))

    everyone = []
    for axis in range(len(group)):
        everyone += [along(axis, step) for step in range(1, group[axis])]

    @pl.when(inner)
    def _():
        greet(everyone + [partner, below, above])

    @pl.when(outer)
    def _():
        greet(
            everyone
            + [inside_next, far_relay, near_relay, relayed_home]
            + [relayed_query, relayed_next, term_relay]
        )

    def columns(h):
        return pl.ds(h * DIM if isinstance(h, int) else pl.multiple_of(h * DIM, DIM), DIM)

    def remote(src, dst, send, recv, device):
        return pltpu.make_async_remote_copy(
            src_ref=src,
            dst_ref=dst,
            send_sem=send,
            recv_sem=recv,
            device_id=device,
            device_id_type=MESH,
        )

    sources = (k_hbm, v_hbm)
    targets = (dk_hbm, dv_hbm)

    def swap_copy(h, i):
        return remote(
            sources[i].at[:, columns(h)], wide.at[h, 1, i],
            swap_send.at[i], kv_recv.at[h, 1, i], partner,
        )

    def first_copy(h, i):
        return remote(
            sources[i].at[:, columns(h)], rel_in.at[h, i],
            swap_send.at[i], rel_recv.at[h, i], far_relay,
        )

    def relay_copies(h, i):
        return [
            remote(
                rel_in.at[h, i], wide.at[h, 1, i],
                relay_send.at[0], kv_recv.at[h, 1, i], relayed_query,
            ),
            remote(
                rel_in.at[h, i], wide.at[h, cross_slot, i],
                relay_send.at[1], kv_recv.at[h, cross_slot, i], relayed_next,
            ),
        ]

    def forward_both(h, i):
        return [
            remote(
                wide.at[h, 1, i], wide.at[h, j, i],
                fwd_send.at[j // 2], kv_recv.at[h, j, i], device,
            )
            for j, device in ((2, below), (0, above))
        ]

    def forward_inside(h, i):
        return [
            remote(
                wide.at[h, 1, i], wide.at[h, fwd_slot, i],
                fwd_send.at[0], kv_recv.at[h, fwd_slot, i], inside_next,
            )
        ]

    def terms_both(h, i):
        return [
            remote(
                term_out.at[h, j, i], term_in.at[h, j, i],
                term_send.at[j], term_recv.at[h, j, i], device,
            )
            for j, device in ((0, below), (1, above))
        ]

    def term_inside(h, i):
        return remote(
            term_out.at[h, in_side, i], term_in.at[h, in_side, i],
            term_send.at[0], term_recv.at[h, in_side, i], inside_next,
        )

    def term_cross(h, i):
        return remote(
            term_out.at[h, cross_side, i], cross_in.at[h, i],
            term_send.at[1], cross_recv.at[h, i], term_relay,
        )

    def term_arrival(h, i):
        return remote(
            term_out.at[h, 0, i], term_in.at[h, cross_side, i],
            term_send.at[0], term_recv.at[h, cross_side, i], inside_next,
        )

    def part_copy(h, i):
        return remote(
            total.at[h, i], part_in.at[h, i],
            part_send.at[0], part_recv.at[h, i], near_relay,
        )

    def final_copy(h, i, src, device):
        return remote(
            src.at[h, i], targets[i].at[:, columns(h)],
            fin_send.at[0], fin_recv.at[i], device,
        )

    def store_copies(h):
        return [
            pltpu.make_async_copy(att_buf.at[h], att_hbm.at[:, columns(h)], store_sem.at[0]),
            pltpu.make_async_copy(dq_buf.at[h], dq_hbm.at[:, columns(h)], store_sem.at[1]),
        ]

    def begin(copies):
        for copy in copies:
            copy.start()

    def arrived(copies):
        for copy in copies:
            copy.wait_recv()

    def sent(copies):
        for copy in copies:
            copy.wait_send()

    def either(relaying, direct):
        pl.when(outer)(relaying)
        pl.when(inner)(direct)

    def send_home(h, i):
        either(lambda: first_copy(h, i).start(), lambda: swap_copy(h, i).start())

    for part in range(AHEAD):
        send_home(part // 2, part % 2)

    for copy in loads:
        copy.wait()

    position = lax.broadcasted_iota(jnp.int32, (1, TOK), 1)
    bias = []
    for j in range(3):
        neighbour = seq + (j - 1)
        inside = jnp.clip(neighbour, 0, BLOCKS - 1)
        open_ = (neighbour == inside) & (flags_ref[j, tower, seq] == 1)
        live = jnp.where(open_, counts_ref[1 - tower, inside], 0)
        bias.append(jnp.where(position < live, 0.0, -1e30).astype(F32))
    bias = jnp.concatenate(bias, axis=1)
    gsum[...] = jnp.zeros_like(gsum)

    def relay(h, i):
        @pl.when(outer)
        def _():
            first_copy(h, i).wait_recv()
            begin(relay_copies(h, i))

    def forward(h, i):
        swap_copy(h, i).wait_recv()
        either(lambda: begin(forward_inside(h, i)), lambda: begin(forward_both(h, i)))

    def send_terms(h, i, left, right):
        terms = dot(left, right, 0, 0).astype(BF)
        term_out[h, 0, i] = terms[:TOK]
        term_mid[h, i] = terms[TOK : 2 * TOK]
        term_out[h, 1, i] = terms[2 * TOK :]
        either(
            lambda: begin([term_inside(h, i), term_cross(h, i)]),
            lambda: begin(terms_both(h, i)),
        )

    def compute(h, i):
        arrived(forward_both(h, i))
        gain = gain_ref[:, columns(h)]
        g = g_buf[:, columns(h)]
        if i == 0:
            q = (q_buf[:, columns(h)].astype(F32) * gain).astype(BF)
            q_scaled[...] = q
            keys = wide[h, :, 0].reshape(WIDE, DIM)
            scores = dot(q, keys, 1, 1) * SCALE + bias
            highest = jnp.max(scores, axis=1, keepdims=True)
            expo = jnp.exp(scores - highest)
            probs = expo / jnp.sum(expo, axis=1, keepdims=True)
            probs_buf[...] = probs
            low = probs.astype(BF)
            low_buf[...] = low
            send_terms(h, 1, low, g)
        else:
            keys = wide[h, :, 0].reshape(WIDE, DIM)
            values = wide[h, :, 1].reshape(WIDE, DIM)
            probs = probs_buf[...]
            dprob = dot(g, values, 1, 1)
            center = jnp.sum(probs * dprob, axis=1, keepdims=True)
            dscore = (probs * (dprob - center) * SCALE).astype(BF)
            send_terms(h, 0, dscore, q_scaled[...])
            att_buf[h] = dot(low_buf[...], values, 1, 0).astype(BF)
            dscaled = dot(dscore, keys, 1, 0)
            dq_buf[h] = (dscaled * gain).astype(BF)
            q_raw = q_buf[:, columns(h)].astype(F32)
            gsum[pl.ds(h, 1), :] = jnp.sum(q_raw * dscaled, axis=0, keepdims=True)
            begin(store_copies(h))

    def gather(h, part):
        i = 1 - part

        def relaying():
            term_arrival(h, i).wait_recv()
            total[h, i] = (
                term_mid[h, i].astype(F32) + term_in[h, cross_side, i].astype(F32)
            ).astype(BF)
            part_copy(h, i).start()

        def direct():
            arrived(terms_both(h, i))
            total[h, i] = (
                term_mid[h, i].astype(F32)
                + term_in[h, 0, i].astype(F32)
                + term_in[h, 1, i].astype(F32)
            ).astype(BF)
            final_copy(h, i, total, partner).start()

        either(relaying, direct)

    def pass_on(h, part):
        i = 1 - part

        @pl.when(outer)
        def _():
            part_copy(h, i).wait_recv()
            term_cross(h, i).wait_recv()
            rel_total[h, i] = (
                part_in[h, i].astype(F32) + cross_in[h, i].astype(F32)
            ).astype(BF)
            final_copy(h, i, rel_total, relayed_home).start()

    stages = (relay, forward, compute, gather, pass_on)

    def advance(step, half):
        for stage, lag in zip((send_home,) + stages, (-AHEAD,) + LAGS):
            h = step + (half - lag) // 2
            part = (half - lag) % 2
            if isinstance(h, int):
                if 0 <= h < HEADS:
                    stage(h, part)
            else:
                pl.when((h >= 0) & (h < HEADS))(functools.partial(stage, h, part))

    looped = (PARTS + LAGS[2] + 1) // 2

    @pl.loop(0, looped)
    def _(step):
        advance(step, 0)
        advance(step, 1)

    def gain_copies(axis):
        return [
            remote(
                gred.at[axis, place[axis]], gred.at[axis, place[axis]],
                gain_send.at[axis, step], gain_recv.at[axis, step], along(axis, step),
            )
            for step in range(1, group[axis])
        ]

    def gain_arrivals(axis):
        return [
            remote(
                gred.at[axis, 0],
                gred.at[axis, (place[axis] + group[axis] - step) % group[axis]],
                gain_send.at[axis, step], gain_recv.at[axis, step], along(axis, step),
            )
            for step in range(1, group[axis])
        ]

    def gain_begin(axis, part):
        gred[axis, place[axis]] = part
        begin(gain_copies(axis))

    def gain_end(axis):
        arrived(gain_arrivals(axis))
        part = gred[axis, 0]
        for slot in range(1, group[axis]):
            part = part + gred[axis, slot]
        return part

    gain_begin(0, gsum[...])
    ended = 0
    for part in range(2 * looped, PARTS + LAGS[4]):
        advance(part // 2, part % 2)
        if ended < 2 and part > 2 * looped:
            gain_begin(ended + 1, gain_end(ended))
            ended += 1
    for axis in range(ended, 2):
        gain_begin(axis + 1, gain_end(axis))

    def all_sent(ref, sems):
        for sem in sems:
            remote(ref, ref, sem, sem, partner).wait_send()

    all_sent(k_hbm, [swap_send.at[0], swap_send.at[1]])
    all_sent(total, [fwd_send.at[0], term_send.at[0], term_send.at[1], fin_send.at[0]])

    @pl.when(outer)
    def _():
        all_sent(total, [relay_send.at[0], relay_send.at[1], part_send.at[0]])

    @pl.when(inner)
    def _():
        all_sent(total, [fwd_send.at[1]])

    for i in range(2):
        pltpu.make_async_copy(att_buf, dq_buf, store_sem.at[i]).wait()

    for i in range(2):
        remote(k_hbm, targets[i], fin_send.at[0], fin_recv.at[i], partner).wait_recv()

    part = gain_end(2)
    for h in range(HEADS):
        gg_ref[:, h * DIM : (h + 1) * DIM] = part[h : h + 1]
    for axis in range(len(group)):
        sent(gain_copies(axis))


def keep(*refs):
    copies = []
    for i in range(4):
        for half in range(2):
            rows = pl.ds(half * 128, 128)
            held = refs[10].at[i, rows]
            copies.append(
                (
                    pltpu.make_async_copy(refs[i].at[rows], held, refs[11].at[0, i, half]),
                    pltpu.make_async_copy(held, refs[i + 5].at[rows], refs[11].at[1, i, half]),
                )
            )
    copies.append(
        (
            pltpu.make_async_copy(refs[4], refs[12], refs[13].at[0]),
            pltpu.make_async_copy(refs[12], refs[9], refs[13].at[1]),
        )
    )
    for load, _ in copies:
        load.start()
    for load, store in copies:
        load.wait()
        store.start()
    for _, store in copies:
        store.wait()


def per_device(query_rows, key_rows, value_rows, out_grad, query_gain, live_counts, intersection):
    anywhere = pl.BlockSpec(memory_space=pl.ANY)
    vmem = pl.BlockSpec(memory_space=pltpu.VMEM)
    block = jax.ShapeDtypeStruct((TOK, WIDTH), BF)
    dma = pltpu.SemaphoreType.DMA
    pair = (HEADS, 2)
    quad = (HEADS, 2, 2)
    shapes = (block, block, block, block, jax.ShapeDtypeStruct((1, WIDTH), F32))
    results = pl.pallas_call(
        kernel,
        out_shape=shapes,
        in_specs=[anywhere] * 7,
        out_specs=(anywhere,) * 4 + (vmem,),
        scratch_shapes=[
            pltpu.VMEM((TOK, WIDTH), BF),
            pltpu.VMEM((TOK, WIDTH), BF),
            pltpu.VMEM((1, WIDTH), F32),
            pltpu.SMEM((2, BLOCKS), jnp.int32),
            pltpu.SMEM((3, 2, BLOCKS), jnp.int32),
            pltpu.VMEM((HEADS, 3, 2, TOK, DIM), BF),
            pltpu.VMEM((HEADS, 2, TOK, DIM), BF),
            pltpu.VMEM((HEADS, 2, 2, TOK, DIM), BF),
            pltpu.VMEM((HEADS, 2, 2, TOK, DIM), BF),
            pltpu.VMEM((HEADS, 2, TOK, DIM), BF),
            pltpu.VMEM((HEADS, 2, TOK, DIM), BF),
            pltpu.VMEM((HEADS, 2, TOK, DIM), BF),
            pltpu.VMEM((HEADS, 2, TOK, DIM), BF),
            pltpu.VMEM((HEADS, 2, TOK, DIM), BF),
            pltpu.VMEM((TOK, WIDE), F32),
            pltpu.VMEM((TOK, WIDE), BF),
            pltpu.VMEM((TOK, DIM), BF),
            pltpu.VMEM((HEADS, TOK, DIM), BF),
            pltpu.VMEM((HEADS, TOK, DIM), BF),
            pltpu.VMEM((16, DIM), F32),
            pltpu.VMEM((3, 8, 16, DIM), F32),
            dma((5,)), dma((2,)), dma(pair), dma((2,)), dma((HEADS, 3, 2)), dma((2,)),
            dma((2,)), dma(quad), dma((1,)), dma(pair), dma(pair),
            dma((1,)), dma((2,)), dma((2,)), dma((3, 8)), dma((3, 8)),
        ],
        compiler_params=pltpu.CompilerParams(
            collective_id=0, has_side_effects=True, vmem_limit_bytes=VMEM_MIB * 2**20
        ),
        name="cross_attention",
    )(
        query_rows[0, 0], key_rows[0, 0], value_rows[0, 0], out_grad[0, 0],
        query_gain, live_counts, jnp.transpose(intersection, (2, 0, 1)),
    )
    results = pl.pallas_call(
        keep,
        out_shape=shapes,
        in_specs=[anywhere] * 5,
        out_specs=(anywhere,) * 5,
        scratch_shapes=[
            pltpu.VMEM((4, TOK, WIDTH), BF), dma((2, 4, 2)),
            pltpu.VMEM((1, WIDTH), F32), dma((2,)),
        ],
        compiler_params=pltpu.CompilerParams(vmem_limit_bytes=VMEM_MIB * 2**20),
        name="keep",
    )(*results)
    shape = (1, 1, TOK, WIDTH)
    return tuple(r.reshape(shape) for r in results[:4]) + (results[4],)


def solution(mesh):
    rows = P("tower", "rep", "seq", None)
    return jax.shard_map(
        per_device,
        mesh=mesh,
        in_specs=(rows, rows, rows, rows, P("tower", None), P(), P()),
        out_specs=(rows, rows, rows, rows, P("tower", None)),
        check_vma=False,
    )
```

```python
import functools
import math

import jax
import jax.numpy as jnp
from jax import lax
from jax.experimental import pallas as pl
from jax.experimental.pallas import tpu as pltpu
from jax.sharding import PartitionSpec as P

HEADS = 12
DIM = 128
TOK = 256
BLOCKS = 64
WIDE = 3 * TOK
WIDTH = HEADS * DIM
SCALE = 1.0 / math.sqrt(DIM)
PARTS = 2 * HEADS
AHEAD = 1
LAGS = (0, 1, 2, 3, 4)
EARLY = 2
VMEM_MIB = 60
MESH = pl.DeviceIdType.MESH
BF = jnp.bfloat16
F32 = jnp.float32


def dot(a, b, ca, cb):
    return lax.dot_general(a, b, (((ca,), (cb,)), ((), ())), preferred_element_type=F32)


def kernel(
    q_hbm, k_hbm, v_hbm, g_hbm, gain_hbm, counts_hbm, flags_hbm,
    att_hbm, dq_hbm, dk_hbm, dv_hbm, gg_ref,
    q_buf, g_buf, gain_ref, counts_ref, flags_ref, wide, rel_in, term_out, term_in, term_mid, total,
    part_in, cross_in, rel_total, probs_buf, low_buf, q_scaled, att_buf, dq_buf, gsum, gred,
    load_sem, swap_send, rel_recv, relay_send, kv_recv, fwd_send,
    term_send, term_recv, part_send, part_recv, cross_recv,
    fin_send, fin_recv, store_sem, gain_send, gain_recv,
):
    tower = lax.axis_index("tower")
    seq = lax.axis_index("seq")
    rep = lax.axis_index("rep")
    x_at, z_at, y_at = seq // 16, (seq // 4) % 4, seq % 4

    first = y_at == 0
    outer = first | (y_at == 3)
    inner = jnp.logical_not(outer)
    side = jnp.where(first, 3, 1)
    toward = jnp.where(first, BLOCKS - 1, 1)
    fwd_slot = jnp.where(first, 0, 2)
    cross_slot = 2 - fwd_slot
    cross_side = jnp.where(first, 0, 1)
    in_side = 1 - cross_side

    early_home = (first & (z_at == 0)) | ((y_at == 3) & (z_at == 3))
    early_relay = (first & (z_at == 3)) | ((y_at == 3) & (z_at == 0))
    home_shift = jnp.where(early_home, EARLY, 0)

    def shifted(block, step):
        return (block + step) % BLOCKS

    def along_z(block, step):
        return (block // 16) * 16 + ((block // 4 + step) % 4) * 4 + block % 4

    partner = (1 - tower, seq, rep)
    below = (tower, shifted(seq, BLOCKS - 1), rep)
    above = (tower, shifted(seq, 1), rep)
    my_relay = along_z(seq, side)
    relayed = along_z(seq, 4 - side)
    far_relay = (1 - tower, my_relay, rep)
    near_relay = (tower, my_relay, rep)
    relayed_home = (1 - tower, relayed, rep)
    relayed_query = (tower, relayed, rep)
    relayed_next = (tower, shifted(relayed, toward), rep)
    inside_next = (tower, shifted(seq, BLOCKS - toward), rep)
    term_relay = (tower, along_z(shifted(seq, toward), 4 - side), rep)

    group = (8, 4, 4)
    place = (y_at * 2 + rep, x_at, z_at)

    def along(axis, step):
        if axis == 0:
            spot = (place[0] + step) % 8
            return (tower, x_at * 16 + z_at * 4 + spot // 2, spot % 2)
        if axis == 1:
            return (tower, ((x_at + step) % 4) * 16 + z_at * 4 + y_at, rep)
        return (tower, along_z(seq, step), rep)

    loads = [
        pltpu.make_async_copy(q_hbm, q_buf, load_sem.at[0]),
        pltpu.make_async_copy(g_hbm, g_buf, load_sem.at[1]),
        pltpu.make_async_copy(gain_hbm, gain_ref, load_sem.at[2]),
        pltpu.make_async_copy(counts_hbm, counts_ref, load_sem.at[3]),
        pltpu.make_async_copy(flags_hbm, flags_ref, load_sem.at[4]),
    ]
    for copy in loads:
        copy.start()

    barrier = pltpu.get_barrier_semaphore()

    def greet(devices):
        for device in devices:
            pl.semaphore_signal(barrier, inc=1, device_id=device, device_id_type=MESH)
        pl.semaphore_wait(barrier, len(devices))

    everyone = []
    for axis in range(len(group)):
        everyone += [along(axis, step) for step in range(1, group[axis])]

    @pl.when(inner)
    def _():
        greet(everyone + [partner, below, above])

    @pl.when(outer)
    def _():
        greet(
            everyone
            + [inside_next, far_relay, near_relay, relayed_home]
            + [relayed_query, relayed_next, term_relay]
        )

    def columns(h):
        return pl.ds(h * DIM if isinstance(h, int) else pl.multiple_of(h * DIM, DIM), DIM)

    def remote(src, dst, send, recv, device):
        return pltpu.make_async_remote_copy(
            src_ref=src,
            dst_ref=dst,
            send_sem=send,
            recv_sem=recv,
            device_id=device,
            device_id_type=MESH,
        )

    sources = (k_hbm, v_hbm)
    targets = (dk_hbm, dv_hbm)

    def swap_copy(h, i):
        return remote(
            sources[i].at[:, columns(h)], wide.at[h, 1, i],
            swap_send.at[i], kv_recv.at[h, 1, i], partner,
        )

    def first_copy(h, i):
        return remote(
            sources[i].at[:, columns(h)], rel_in.at[h, i],
            swap_send.at[i], rel_recv.at[h, i], far_relay,
        )

    def relay_copies(h, i):
        return [
            remote(
                rel_in.at[h, i], wide.at[h, 1, i],
                relay_send.at[0], kv_recv.at[h, 1, i], relayed_query,
            ),
            remote(
                rel_in.at[h, i], wide.at[h, cross_slot, i],
                relay_send.at[1], kv_recv.at[h, cross_slot, i], relayed_next,
            ),
        ]

    def forward_both(h, i):
        return [
            remote(
                wide.at[h, 1, i], wide.at[h, j, i],
                fwd_send.at[j // 2], kv_recv.at[h, j, i], device,
            )
            for j, device in ((2, below), (0, above))
        ]

    def forward_inside(h, i):
        return [
            remote(
                wide.at[h, 1, i], wide.at[h, fwd_slot, i],
                fwd_send.at[0], kv_recv.at[h, fwd_slot, i], inside_next,
            )
        ]

    def terms_both(h, i):
        return [
            remote(
                term_out.at[h, j, i], term_in.at[h, j, i],
                term_send.at[j], term_recv.at[h, j, i], device,
            )
            for j, device in ((0, below), (1, above))
        ]

    def term_inside(h, i):
        return remote(
            term_out.at[h, in_side, i], term_in.at[h, in_side, i],
            term_send.at[0], term_recv.at[h, in_side, i], inside_next,
        )

    def term_cross(h, i):
        return remote(
            term_out.at[h, cross_side, i], cross_in.at[h, i],
            term_send.at[1], cross_recv.at[h, i], term_relay,
        )

    def term_arrival(h, i):
        return remote(
            term_out.at[h, 0, i], term_in.at[h, cross_side, i],
            term_send.at[0], term_recv.at[h, cross_side, i], inside_next,
        )

    def part_copy(h, i):
        return remote(
            total.at[h, i], part_in.at[h, i],
            part_send.at[0], part_recv.at[h, i], near_relay,
        )

    def final_copy(h, i, src, device):
        return remote(
            src.at[h, i], targets[i].at[:, columns(h)],
            fin_send.at[0], fin_recv.at[i], device,
        )

    def store_copies(h):
        return [
            pltpu.make_async_copy(att_buf.at[h], att_hbm.at[:, columns(h)], store_sem.at[0]),
            pltpu.make_async_copy(dq_buf.at[h], dq_hbm.at[:, columns(h)], store_sem.at[1]),
        ]

    def begin(copies):
        for copy in copies:
            copy.start()

    def arrived(copies):
        for copy in copies:
            copy.wait_recv()

    def sent(copies):
        for copy in copies:
            copy.wait_send()

    def either(relaying, direct):
        pl.when(outer)(relaying)
        pl.when(inner)(direct)

    def send_home(h, i):
        either(lambda: first_copy(h, i).start(), lambda: swap_copy(h, i).start())

    for part in range(AHEAD):
        send_home(part // 2, part % 2)

    @pl.when(early_home)
    def _():
        for part in range(AHEAD, AHEAD + 2 * EARLY):
            first_copy(part // 2, part % 2).start()

    for copy in loads:
        copy.wait()

    position = lax.broadcasted_iota(jnp.int32, (1, TOK), 1)
    bias = []
    for j in range(3):
        neighbour = seq + (j - 1)
        inside = jnp.clip(neighbour, 0, BLOCKS - 1)
        open_ = (neighbour == inside) & (flags_ref[j, tower, seq] == 1)
        live = jnp.where(open_, counts_ref[1 - tower, inside], 0)
        bias.append(jnp.where(position < live, 0.0, -1e30).astype(F32))
    bias = jnp.concatenate(bias, axis=1)
    gsum[...] = jnp.zeros_like(gsum)

    def relay(h, i):
        @pl.when(outer)
        def _():
            first_copy(h, i).wait_recv()
            begin(relay_copies(h, i))

    def forward(h, i):
        swap_copy(h, i).wait_recv()
        either(lambda: begin(forward_inside(h, i)), lambda: begin(forward_both(h, i)))

    def send_terms(h, i, left, right):
        terms = dot(left, right, 0, 0).astype(BF)
        term_out[h, 0, i] = terms[:TOK]
        term_mid[h, i] = terms[TOK : 2 * TOK]
        term_out[h, 1, i] = terms[2 * TOK :]
        either(
            lambda: begin([term_inside(h, i), term_cross(h, i)]),
            lambda: begin(terms_both(h, i)),
        )

    def compute(h, i):
        arrived(forward_both(h, i))
        gain = gain_ref[:, columns(h)]
        g = g_buf[:, columns(h)]
        if i == 0:
            q = (q_buf[:, columns(h)].astype(F32) * gain).astype(BF)
            q_scaled[...] = q
            keys = wide[h, :, 0].reshape(WIDE, DIM)
            scores = dot(q, keys, 1, 1) * SCALE + bias
            highest = jnp.max(scores, axis=1, keepdims=True)
            expo = jnp.exp(scores - highest)
            probs = expo / jnp.sum(expo, axis=1, keepdims=True)
            probs_buf[...] = probs
            low = probs.astype(BF)
            low_buf[...] = low
            send_terms(h, 1, low, g)
        else:
            keys = wide[h, :, 0].reshape(WIDE, DIM)
            values = wide[h, :, 1].reshape(WIDE, DIM)
            probs = probs_buf[...]
            dprob = dot(g, values, 1, 1)
            center = jnp.sum(probs * dprob, axis=1, keepdims=True)
            dscore = (probs * (dprob - center) * SCALE).astype(BF)
            send_terms(h, 0, dscore, q_scaled[...])
            att_buf[h] = dot(low_buf[...], values, 1, 0).astype(BF)
            dscaled = dot(dscore, keys, 1, 0)
            dq_buf[h] = (dscaled * gain).astype(BF)
            q_raw = q_buf[:, columns(h)].astype(F32)
            gsum[pl.ds(h, 1), :] = jnp.sum(q_raw * dscaled, axis=0, keepdims=True)
            begin(store_copies(h))

    def gather(h, part):
        i = 1 - part

        def relaying():
            term_arrival(h, i).wait_recv()
            total[h, i] = (
                term_mid[h, i].astype(F32) + term_in[h, cross_side, i].astype(F32)
            ).astype(BF)
            part_copy(h, i).start()

        def direct():
            arrived(terms_both(h, i))
            total[h, i] = (
                term_mid[h, i].astype(F32)
                + term_in[h, 0, i].astype(F32)
                + term_in[h, 1, i].astype(F32)
            ).astype(BF)
            final_copy(h, i, total, partner).start()

        either(relaying, direct)

    def pass_on(h, part):
        i = 1 - part

        @pl.when(outer)
        def _():
            part_copy(h, i).wait_recv()
            term_cross(h, i).wait_recv()
            rel_total[h, i] = (
                part_in[h, i].astype(F32) + cross_in[h, i].astype(F32)
            ).astype(BF)
            final_copy(h, i, rel_total, relayed_home).start()

    def relay_early(step, half):
        @pl.when(early_relay & (step < EARLY))
        def _():
            for i in range(2):
                relay(2 * step + half, i)

        @pl.when(early_relay & (step >= EARLY) & (step < HEADS - EARLY))
        def _():
            relay(step + EARLY, half)

    stages = (forward, compute, gather, pass_on)

    def advance(step, half):
        if not isinstance(step, int):
            h = step + (half + AHEAD) // 2 + home_shift
            pl.when(h < HEADS)(functools.partial(send_home, h, (half + AHEAD) % 2))
            relay_early(step, half)
            pl.when(jnp.logical_not(early_relay) & (step < HEADS))(
                functools.partial(relay, step, half)
            )
        for stage, lag in zip(stages, LAGS[1:]):
            h = step + (half - lag) // 2
            part = (half - lag) % 2
            if isinstance(h, int):
                if 0 <= h < HEADS:
                    stage(h, part)
            else:
                pl.when((h >= 0) & (h < HEADS))(functools.partial(stage, h, part))

    looped = (PARTS + LAGS[2] + 1) // 2

    @pl.loop(0, looped)
    def _(step):
        advance(step, 0)
        advance(step, 1)

    def gain_copies(axis):
        return [
            remote(
                gred.at[axis, place[axis]], gred.at[axis, place[axis]],
                gain_send.at[axis, step], gain_recv.at[axis, step], along(axis, step),
            )
            for step in range(1, group[axis])
        ]

    def gain_arrivals(axis):
        return [
            remote(
                gred.at[axis, 0],
                gred.at[axis, (place[axis] + group[axis] - step) % group[axis]],
                gain_send.at[axis, step], gain_recv.at[axis, step], along(axis, step),
            )
            for step in range(1, group[axis])
        ]

    def gain_begin(axis, part):
        gred[axis, place[axis]] = part
        begin(gain_copies(axis))

    def gain_end(axis):
        arrived(gain_arrivals(axis))
        part = gred[axis, 0]
        for slot in range(1, group[axis]):
            part = part + gred[axis, slot]
        return part

    gain_begin(0, gsum[...])
    ended = 0
    for part in range(2 * looped, PARTS + LAGS[4]):
        advance(part // 2, part % 2)
        if ended < 2 and part > 2 * looped:
            gain_begin(ended + 1, gain_end(ended))
            ended += 1
    for axis in range(ended, 2):
        gain_begin(axis + 1, gain_end(axis))

    def all_sent(ref, sems):
        for sem in sems:
            remote(ref, ref, sem, sem, partner).wait_send()

    all_sent(k_hbm, [swap_send.at[0], swap_send.at[1]])
    all_sent(total, [fwd_send.at[0], term_send.at[0], term_send.at[1], fin_send.at[0]])

    @pl.when(outer)
    def _():
        all_sent(total, [relay_send.at[0], relay_send.at[1], part_send.at[0]])

    @pl.when(inner)
    def _():
        all_sent(total, [fwd_send.at[1]])

    for i in range(2):
        pltpu.make_async_copy(att_buf, dq_buf, store_sem.at[i]).wait()

    for i in range(2):
        remote(k_hbm, targets[i], fin_send.at[0], fin_recv.at[i], partner).wait_recv()

    part = gain_end(2)
    for h in range(HEADS):
        gg_ref[:, h * DIM : (h + 1) * DIM] = part[h : h + 1]
    for axis in range(len(group)):
        sent(gain_copies(axis))


def keep(*refs):
    copies = []
    for i in range(4):
        for half in range(2):
            rows = pl.ds(half * 128, 128)
            held = refs[10].at[i, rows]
            copies.append(
                (
                    pltpu.make_async_copy(refs[i].at[rows], held, refs[11].at[0, i, half]),
                    pltpu.make_async_copy(held, refs[i + 5].at[rows], refs[11].at[1, i, half]),
                )
            )
    copies.append(
        (
            pltpu.make_async_copy(refs[4], refs[12], refs[13].at[0]),
            pltpu.make_async_copy(refs[12], refs[9], refs[13].at[1]),
        )
    )
    for load, _ in copies:
        load.start()
    for load, store in copies:
        load.wait()
        store.start()
    for _, store in copies:
        store.wait()


def per_device(query_rows, key_rows, value_rows, out_grad, query_gain, live_counts, intersection):
    anywhere = pl.BlockSpec(memory_space=pl.ANY)
    vmem = pl.BlockSpec(memory_space=pltpu.VMEM)
    block = jax.ShapeDtypeStruct((TOK, WIDTH), BF)
    dma = pltpu.SemaphoreType.DMA
    pair = (HEADS, 2)
    quad = (HEADS, 2, 2)
    shapes = (block, block, block, block, jax.ShapeDtypeStruct((1, WIDTH), F32))
    results = pl.pallas_call(
        kernel,
        out_shape=shapes,
        in_specs=[anywhere] * 7,
        out_specs=(anywhere,) * 4 + (vmem,),
        scratch_shapes=[
            pltpu.VMEM((TOK, WIDTH), BF),
            pltpu.VMEM((TOK, WIDTH), BF),
            pltpu.VMEM((1, WIDTH), F32),
            pltpu.SMEM((2, BLOCKS), jnp.int32),
            pltpu.SMEM((3, 2, BLOCKS), jnp.int32),
            pltpu.VMEM((HEADS, 3, 2, TOK, DIM), BF),
            pltpu.VMEM((HEADS, 2, TOK, DIM), BF),
            pltpu.VMEM((HEADS, 2, 2, TOK, DIM), BF),
            pltpu.VMEM((HEADS, 2, 2, TOK, DIM), BF),
            pltpu.VMEM((HEADS, 2, TOK, DIM), BF),
            pltpu.VMEM((HEADS, 2, TOK, DIM), BF),
            pltpu.VMEM((HEADS, 2, TOK, DIM), BF),
            pltpu.VMEM((HEADS, 2, TOK, DIM), BF),
            pltpu.VMEM((HEADS, 2, TOK, DIM), BF),
            pltpu.VMEM((TOK, WIDE), F32),
            pltpu.VMEM((TOK, WIDE), BF),
            pltpu.VMEM((TOK, DIM), BF),
            pltpu.VMEM((HEADS, TOK, DIM), BF),
            pltpu.VMEM((HEADS, TOK, DIM), BF),
            pltpu.VMEM((16, DIM), F32),
            pltpu.VMEM((3, 8, 16, DIM), F32),
            dma((5,)), dma((2,)), dma(pair), dma((2,)), dma((HEADS, 3, 2)), dma((2,)),
            dma((2,)), dma(quad), dma((1,)), dma(pair), dma(pair),
            dma((1,)), dma((2,)), dma((2,)), dma((3, 8)), dma((3, 8)),
        ],
        compiler_params=pltpu.CompilerParams(
            collective_id=0, has_side_effects=True, vmem_limit_bytes=VMEM_MIB * 2**20
        ),
        name="cross_attention",
    )(
        query_rows[0, 0], key_rows[0, 0], value_rows[0, 0], out_grad[0, 0],
        query_gain, live_counts, jnp.transpose(intersection, (2, 0, 1)),
    )
    results = pl.pallas_call(
        keep,
        out_shape=shapes,
        in_specs=[anywhere] * 5,
        out_specs=(anywhere,) * 5,
        scratch_shapes=[
            pltpu.VMEM((4, TOK, WIDTH), BF), dma((2, 4, 2)),
            pltpu.VMEM((1, WIDTH), F32), dma((2,)),
        ],
        compiler_params=pltpu.CompilerParams(vmem_limit_bytes=VMEM_MIB * 2**20),
        name="keep",
    )(*results)
    shape = (1, 1, TOK, WIDTH)
    return tuple(r.reshape(shape) for r in results[:4]) + (results[4],)


def solution(mesh):
    rows = P("tower", "rep", "seq", None)
    return jax.shard_map(
        per_device,
        mesh=mesh,
        in_specs=(rows, rows, rows, rows, P("tower", None), P(), P()),
        out_specs=(rows, rows, rows, rows, P("tower", None)),
        check_vma=False,
    )
```

```python
import functools
import math

import jax
import jax.numpy as jnp
from jax import lax
from jax.experimental import pallas as pl
from jax.experimental.pallas import tpu as pltpu
from jax.sharding import PartitionSpec as P

HEADS = 12
DIM = 128
TOK = 256
BLOCKS = 64
WIDE = 3 * TOK
WIDTH = HEADS * DIM
SCALE = 1.0 / math.sqrt(DIM)
PARTS = 2 * HEADS
AHEAD = 1
LAGS = (0, 1, 2, 3, 4)
EARLY = 3
LATE = 1
VMEM_MIB = 60
MESH = pl.DeviceIdType.MESH
BF = jnp.bfloat16
F32 = jnp.float32


def dot(a, b, ca, cb):
    return lax.dot_general(a, b, (((ca,), (cb,)), ((), ())), preferred_element_type=F32)


def kernel(
    q_hbm, k_hbm, v_hbm, g_hbm, gain_hbm, counts_hbm, flags_hbm,
    att_hbm, dq_hbm, dk_hbm, dv_hbm, gg_hbm,
    q_buf, g_buf, gain_ref, counts_ref, flags_ref, wide, rel_in, term_out, term_in, term_mid, total,
    part_in, cross_in, rel_total, probs_buf, low_buf, q_scaled, att_buf, dq_buf, gsum, gred, gg_ref,
    load_sem, swap_send, rel_recv, relay_send, kv_recv, fwd_send,
    term_send, term_recv, part_send, part_recv, cross_recv,
    fin_send, fin_recv, store_sem, gain_send, gain_recv,
):
    tower = lax.axis_index("tower")
    seq = lax.axis_index("seq")
    rep = lax.axis_index("rep")
    x_at, z_at, y_at = seq // 16, (seq // 4) % 4, seq % 4

    first = y_at == 0
    outer = first | (y_at == 3)
    inner = jnp.logical_not(outer)
    side = jnp.where(first, 3, 1)
    toward = jnp.where(first, BLOCKS - 1, 1)
    fwd_slot = jnp.where(first, 0, 2)
    cross_slot = 2 - fwd_slot
    cross_side = jnp.where(first, 0, 1)
    in_side = 1 - cross_side

    early_home = (first & (z_at == 0)) | ((y_at == 3) & (z_at == 3))
    early_relay = (first & (z_at == 3)) | ((y_at == 3) & (z_at == 0))
    home_shift = jnp.where(early_home, EARLY, 0)
    pass_shift = jnp.where(early_relay, LATE, 0)

    def shifted(block, step):
        return (block + step) % BLOCKS

    def along_z(block, step):
        return (block // 16) * 16 + ((block // 4 + step) % 4) * 4 + block % 4

    partner = (1 - tower, seq, rep)
    below = (tower, shifted(seq, BLOCKS - 1), rep)
    above = (tower, shifted(seq, 1), rep)
    my_relay = along_z(seq, side)
    relayed = along_z(seq, 4 - side)
    far_relay = (1 - tower, my_relay, rep)
    near_relay = (tower, my_relay, rep)
    relayed_home = (1 - tower, relayed, rep)
    relayed_query = (tower, relayed, rep)
    relayed_next = (tower, shifted(relayed, toward), rep)
    inside_next = (tower, shifted(seq, BLOCKS - toward), rep)
    term_relay = (tower, along_z(shifted(seq, toward), 4 - side), rep)

    group = (8, 4, 4)
    place = (y_at * 2 + rep, x_at, z_at)

    def along(axis, step):
        if axis == 0:
            spot = (place[0] + step) % 8
            return (tower, x_at * 16 + z_at * 4 + spot // 2, spot % 2)
        if axis == 1:
            return (tower, ((x_at + step) % 4) * 16 + z_at * 4 + y_at, rep)
        return (tower, along_z(seq, step), rep)

    loads = [
        pltpu.make_async_copy(q_hbm, q_buf, load_sem.at[0]),
        pltpu.make_async_copy(g_hbm, g_buf, load_sem.at[1]),
        pltpu.make_async_copy(gain_hbm, gain_ref, load_sem.at[2]),
        pltpu.make_async_copy(counts_hbm, counts_ref, load_sem.at[3]),
        pltpu.make_async_copy(flags_hbm, flags_ref, load_sem.at[4]),
    ]
    for copy in loads:
        copy.start()

    barrier = pltpu.get_barrier_semaphore()

    def greet(devices):
        for device in devices:
            pl.semaphore_signal(barrier, inc=1, device_id=device, device_id_type=MESH)
        pl.semaphore_wait(barrier, len(devices))

    everyone = []
    for axis in range(len(group)):
        everyone += [along(axis, step) for step in range(1, group[axis])]

    @pl.when(inner)
    def _():
        greet(everyone + [partner, below, above])

    @pl.when(outer)
    def _():
        greet(
            everyone
            + [inside_next, far_relay, near_relay, relayed_home]
            + [relayed_query, relayed_next, term_relay]
        )

    def columns(h):
        return pl.ds(h * DIM if isinstance(h, int) else pl.multiple_of(h * DIM, DIM), DIM)

    def remote(src, dst, send, recv, device):
        return pltpu.make_async_remote_copy(
            src_ref=src,
            dst_ref=dst,
            send_sem=send,
            recv_sem=recv,
            device_id=device,
            device_id_type=MESH,
        )

    sources = (k_hbm, v_hbm)
    targets = (dk_hbm, dv_hbm)

    def swap_copy(h, i):
        return remote(
            sources[i].at[:, columns(h)], wide.at[h, 1, i],
            swap_send.at[i], kv_recv.at[h, 1, i], partner,
        )

    def first_copy(h, i):
        return remote(
            sources[i].at[:, columns(h)], rel_in.at[h, i],
            swap_send.at[i], rel_recv.at[h, i], far_relay,
        )

    def relay_copies(h, i):
        return [
            remote(
                rel_in.at[h, i], wide.at[h, 1, i],
                relay_send.at[0], kv_recv.at[h, 1, i], relayed_query,
            ),
            remote(
                rel_in.at[h, i], wide.at[h, cross_slot, i],
                relay_send.at[1], kv_recv.at[h, cross_slot, i], relayed_next,
            ),
        ]

    def forward_both(h, i):
        return [
            remote(
                wide.at[h, 1, i], wide.at[h, j, i],
                fwd_send.at[j // 2], kv_recv.at[h, j, i], device,
            )
            for j, device in ((2, below), (0, above))
        ]

    def forward_inside(h, i):
        return [
            remote(
                wide.at[h, 1, i], wide.at[h, fwd_slot, i],
                fwd_send.at[0], kv_recv.at[h, fwd_slot, i], inside_next,
            )
        ]

    def terms_both(h, i):
        return [
            remote(
                term_out.at[h, j, i], term_in.at[h, j, i],
                term_send.at[j], term_recv.at[h, j, i], device,
            )
            for j, device in ((0, below), (1, above))
        ]

    def term_inside(h, i):
        return remote(
            term_out.at[h, in_side, i], term_in.at[h, in_side, i],
            term_send.at[0], term_recv.at[h, in_side, i], inside_next,
        )

    def term_cross(h, i):
        return remote(
            term_out.at[h, cross_side, i], cross_in.at[h, i],
            term_send.at[1], cross_recv.at[h, i], term_relay,
        )

    def term_arrival(h, i):
        return remote(
            term_out.at[h, 0, i], term_in.at[h, cross_side, i],
            term_send.at[0], term_recv.at[h, cross_side, i], inside_next,
        )

    def part_copy(h, i):
        return remote(
            total.at[h, i], part_in.at[h, i],
            part_send.at[0], part_recv.at[h, i], near_relay,
        )

    def final_copy(h, i, src, device):
        return remote(
            src.at[h, i], targets[i].at[:, columns(h)],
            fin_send.at[0], fin_recv.at[i], device,
        )

    def store_copies(h):
        return [
            pltpu.make_async_copy(att_buf.at[h], att_hbm.at[:, columns(h)], store_sem.at[0]),
            pltpu.make_async_copy(dq_buf.at[h], dq_hbm.at[:, columns(h)], store_sem.at[1]),
        ]

    def begin(copies):
        for copy in copies:
            copy.start()

    def arrived(copies):
        for copy in copies:
            copy.wait_recv()

    def sent(copies):
        for copy in copies:
            copy.wait_send()

    def either(relaying, direct):
        pl.when(outer)(relaying)
        pl.when(inner)(direct)

    def send_home(h, i):
        either(lambda: first_copy(h, i).start(), lambda: swap_copy(h, i).start())

    for part in range(AHEAD):
        send_home(part // 2, part % 2)

    @pl.when(early_home)
    def _():
        for part in range(AHEAD, AHEAD + 2 * EARLY):
            first_copy(part // 2, part % 2).start()

    for copy in loads:
        copy.wait()

    position = lax.broadcasted_iota(jnp.int32, (1, TOK), 1)
    bias = []
    for j in range(3):
        neighbour = seq + (j - 1)
        inside = jnp.clip(neighbour, 0, BLOCKS - 1)
        open_ = (neighbour == inside) & (flags_ref[j, tower, seq] == 1)
        live = jnp.where(open_, counts_ref[1 - tower, inside], 0)
        bias.append(jnp.where(position < live, 0.0, -1e30).astype(F32))
    bias = jnp.concatenate(bias, axis=1)
    gsum[...] = jnp.zeros_like(gsum)

    def relay(h, i):
        @pl.when(outer)
        def _():
            first_copy(h, i).wait_recv()
            begin(relay_copies(h, i))

    def forward(h, i):
        swap_copy(h, i).wait_recv()
        either(lambda: begin(forward_inside(h, i)), lambda: begin(forward_both(h, i)))

    def send_terms(h, i, left, right):
        terms = dot(left, right, 0, 0).astype(BF)
        term_out[h, 0, i] = terms[:TOK]
        term_mid[h, i] = terms[TOK : 2 * TOK]
        term_out[h, 1, i] = terms[2 * TOK :]
        either(
            lambda: begin([term_inside(h, i), term_cross(h, i)]),
            lambda: begin(terms_both(h, i)),
        )

    def compute(h, i):
        arrived(forward_both(h, i))
        gain = gain_ref[:, columns(h)]
        g = g_buf[:, columns(h)]
        if i == 0:
            q = (q_buf[:, columns(h)].astype(F32) * gain).astype(BF)
            q_scaled[...] = q
            keys = wide[h, :, 0].reshape(WIDE, DIM)
            scores = dot(q, keys, 1, 1) * SCALE + bias
            highest = jnp.max(scores, axis=1, keepdims=True)
            expo = jnp.exp(scores - highest)
            probs = expo / jnp.sum(expo, axis=1, keepdims=True)
            probs_buf[...] = probs
            low = probs.astype(BF)
            low_buf[...] = low
            send_terms(h, 1, low, g)
        else:
            keys = wide[h, :, 0].reshape(WIDE, DIM)
            values = wide[h, :, 1].reshape(WIDE, DIM)
            probs = probs_buf[...]
            dprob = dot(g, values, 1, 1)
            center = jnp.sum(probs * dprob, axis=1, keepdims=True)
            dscore = (probs * (dprob - center) * SCALE).astype(BF)
            send_terms(h, 0, dscore, q_scaled[...])
            att_buf[h] = dot(low_buf[...], values, 1, 0).astype(BF)
            dscaled = dot(dscore, keys, 1, 0)
            dq_buf[h] = (dscaled * gain).astype(BF)
            q_raw = q_buf[:, columns(h)].astype(F32)
            gsum[pl.ds(h, 1), :] = jnp.sum(q_raw * dscaled, axis=0, keepdims=True)
            begin(store_copies(h))

    def gather(h, part):
        i = 1 - part

        def relaying():
            term_arrival(h, i).wait_recv()
            total[h, i] = (
                term_mid[h, i].astype(F32) + term_in[h, cross_side, i].astype(F32)
            ).astype(BF)
            part_copy(h, i).start()

        def direct():
            arrived(terms_both(h, i))
            total[h, i] = (
                term_mid[h, i].astype(F32)
                + term_in[h, 0, i].astype(F32)
                + term_in[h, 1, i].astype(F32)
            ).astype(BF)
            final_copy(h, i, total, partner).start()

        either(relaying, direct)

    def pass_on(h, part):
        i = 1 - part

        @pl.when(outer)
        def _():
            part_copy(h, i).wait_recv()
            term_cross(h, i).wait_recv()
            rel_total[h, i] = (
                part_in[h, i].astype(F32) + cross_in[h, i].astype(F32)
            ).astype(BF)
            final_copy(h, i, rel_total, relayed_home).start()

    def relay_early(step, half):
        @pl.when(early_relay & (step < EARLY))
        def _():
            for i in range(2):
                relay(2 * step + half, i)

        @pl.when(early_relay & (step >= EARLY) & (step < HEADS - EARLY))
        def _():
            relay(step + EARLY, half)

    stages = (forward, compute, gather, pass_on)

    def advance(step, half):
        h = step + (half + AHEAD) // 2 + home_shift
        pl.when(h < HEADS)(functools.partial(send_home, h, (half + AHEAD) % 2))
        relay_early(step, half)
        pl.when(jnp.logical_not(early_relay) & (step < HEADS))(
            functools.partial(relay, step, half)
        )
        for stage, lag in zip((forward, compute), LAGS[1:3]):
            h = step + (half - lag) // 2
            pl.when((h >= 0) & (h < HEADS))(functools.partial(stage, h, (half - lag) % 2))
        for stage, lag, shift in ((gather, LAGS[3], 0), (pass_on, LAGS[4], pass_shift)):
            h = step + (half - lag) // 2 - shift
            pl.when((h >= 0) & (h < HEADS))(functools.partial(stage, h, (half - lag) % 2))

    def conclude(first_part):
        for part in range(first_part - LAGS[3], PARTS):
            gather(part // 2, part % 2)
        yield
        for part in range(first_part - LAGS[4] - 2 * LATE, PARTS):
            run = functools.partial(pass_on, part // 2, part % 2)
            if part < first_part - LAGS[4]:
                pl.when(early_relay)(run)
            else:
                run()
        yield

    looped = (PARTS + LAGS[2] + 1) // 2

    @pl.loop(0, looped)
    def _(step):
        advance(step, 0)
        advance(step, 1)

    def gain_copies(axis):
        return [
            remote(
                gred.at[axis, place[axis]], gred.at[axis, place[axis]],
                gain_send.at[axis, step], gain_recv.at[axis, step], along(axis, step),
            )
            for step in range(1, group[axis])
        ]

    def gain_arrivals(axis):
        return [
            remote(
                gred.at[axis, 0],
                gred.at[axis, (place[axis] + group[axis] - step) % group[axis]],
                gain_send.at[axis, step], gain_recv.at[axis, step], along(axis, step),
            )
            for step in range(1, group[axis])
        ]

    def gain_begin(axis, part):
        gred[axis, place[axis]] = part
        begin(gain_copies(axis))

    def gain_end(axis):
        arrived(gain_arrivals(axis))
        part = gred[axis, 0]
        for slot in range(1, group[axis]):
            part = part + gred[axis, slot]
        return part

    gain_begin(0, gsum[...])
    for axis, _ in enumerate(conclude(2 * looped)):
        gain_begin(axis + 1, gain_end(axis))

    def all_sent(ref, sems):
        for sem in sems:
            remote(ref, ref, sem, sem, partner).wait_send()

    all_sent(k_hbm, [swap_send.at[0], swap_send.at[1]])
    all_sent(total, [fwd_send.at[0], term_send.at[0], term_send.at[1], fin_send.at[0]])

    @pl.when(outer)
    def _():
        all_sent(total, [relay_send.at[0], relay_send.at[1], part_send.at[0]])

    @pl.when(inner)
    def _():
        all_sent(total, [fwd_send.at[1]])

    for i in range(2):
        pltpu.make_async_copy(att_buf, dq_buf, store_sem.at[i]).wait()

    part = gain_end(2)
    for h in range(HEADS):
        gg_ref[:, h * DIM : (h + 1) * DIM] = part[h : h + 1]
    gg_copy = pltpu.make_async_copy(gg_ref, gg_hbm, load_sem.at[5])
    gg_copy.start()
    for axis in range(len(group)):
        sent(gain_copies(axis))

    for i in range(2):
        remote(k_hbm, targets[i], fin_send.at[0], fin_recv.at[i], partner).wait_recv()

    gg_copy.wait()


def keep(*refs):
    copies = []
    for i in range(4):
        for half in range(4):
            rows = pl.ds(half * 64, 64)
            held = refs[10].at[i, rows]
            copies.append(
                (
                    pltpu.make_async_copy(refs[i].at[rows], held, refs[11].at[0, i, half]),
                    pltpu.make_async_copy(held, refs[i + 5].at[rows], refs[11].at[1, i, half]),
                )
            )
    copies.append(
        (
            pltpu.make_async_copy(refs[4], refs[12], refs[13].at[0]),
            pltpu.make_async_copy(refs[12], refs[9], refs[13].at[1]),
        )
    )
    for load, _ in copies:
        load.start()
    for load, store in copies:
        load.wait()
        store.start()
    for _, store in copies:
        store.wait()


def per_device(query_rows, key_rows, value_rows, out_grad, query_gain, live_counts, intersection):
    anywhere = pl.BlockSpec(memory_space=pl.ANY)
    block = jax.ShapeDtypeStruct((TOK, WIDTH), BF)
    dma = pltpu.SemaphoreType.DMA
    pair = (HEADS, 2)
    quad = (HEADS, 2, 2)
    shapes = (block, block, block, block, jax.ShapeDtypeStruct((1, WIDTH), F32))
    results = pl.pallas_call(
        kernel,
        out_shape=shapes,
        in_specs=[anywhere] * 7,
        out_specs=(anywhere,) * 5,
        scratch_shapes=[
            pltpu.VMEM((TOK, WIDTH), BF),
            pltpu.VMEM((TOK, WIDTH), BF),
            pltpu.VMEM((1, WIDTH), F32),
            pltpu.SMEM((2, BLOCKS), jnp.int32),
            pltpu.SMEM((3, 2, BLOCKS), jnp.int32),
            pltpu.VMEM((HEADS, 3, 2, TOK, DIM), BF),
            pltpu.VMEM((HEADS, 2, TOK, DIM), BF),
            pltpu.VMEM((HEADS, 2, 2, TOK, DIM), BF),
            pltpu.VMEM((HEADS, 2, 2, TOK, DIM), BF),
            pltpu.VMEM((HEADS, 2, TOK, DIM), BF),
            pltpu.VMEM((HEADS, 2, TOK, DIM), BF),
            pltpu.VMEM((HEADS, 2, TOK, DIM), BF),
            pltpu.VMEM((HEADS, 2, TOK, DIM), BF),
            pltpu.VMEM((HEADS, 2, TOK, DIM), BF),
            pltpu.VMEM((TOK, WIDE), F32),
            pltpu.VMEM((TOK, WIDE), BF),
            pltpu.VMEM((TOK, DIM), BF),
            pltpu.VMEM((HEADS, TOK, DIM), BF),
            pltpu.VMEM((HEADS, TOK, DIM), BF),
            pltpu.VMEM((16, DIM), F32),
            pltpu.VMEM((3, 8, 16, DIM), F32),
            pltpu.VMEM((1, WIDTH), F32),
            dma((6,)), dma((2,)), dma(pair), dma((2,)), dma((HEADS, 3, 2)), dma((2,)),
            dma((2,)), dma(quad), dma((1,)), dma(pair), dma(pair),
            dma((1,)), dma((2,)), dma((2,)), dma((3, 8)), dma((3, 8)),
        ],
        compiler_params=pltpu.CompilerParams(
            collective_id=0, has_side_effects=True, vmem_limit_bytes=VMEM_MIB * 2**20
        ),
        name="cross_attention",
    )(
        query_rows[0, 0], key_rows[0, 0], value_rows[0, 0], out_grad[0, 0],
        query_gain, live_counts, jnp.transpose(intersection, (2, 0, 1)),
    )
    results = pl.pallas_call(
        keep,
        out_shape=shapes,
        in_specs=[anywhere] * 5,
        out_specs=(anywhere,) * 5,
        scratch_shapes=[
            pltpu.VMEM((4, TOK, WIDTH), BF), dma((2, 4, 4)),
            pltpu.VMEM((1, WIDTH), F32), dma((2,)),
        ],
        compiler_params=pltpu.CompilerParams(vmem_limit_bytes=VMEM_MIB * 2**20),
        name="keep",
    )(*results)
    shape = (1, 1, TOK, WIDTH)
    return tuple(r.reshape(shape) for r in results[:4]) + (results[4],)


def solution(mesh):
    rows = P("tower", "rep", "seq", None)
    return jax.shard_map(
        per_device,
        mesh=mesh,
        in_specs=(rows, rows, rows, rows, P("tower", None), P(), P()),
        out_specs=(rows, rows, rows, rows, P("tower", None)),
        check_vma=False,
    )
```

```python
import functools
import math

import jax
import jax.numpy as jnp
from jax import lax
from jax.experimental import pallas as pl
from jax.experimental.pallas import tpu as pltpu
from jax.sharding import PartitionSpec as P

HEADS = 12
DIM = 128
TOK = 256
BLOCKS = 64
WIDE = 3 * TOK
WIDTH = HEADS * DIM
SCALE = 1.0 / math.sqrt(DIM)
PARTS = 2 * HEADS
AHEAD = 2
LAGS = (0, 1, 2, 3, 4)
EARLY = 3
LATE = 1
VMEM_MIB = 60
MESH = pl.DeviceIdType.MESH
BF = jnp.bfloat16
F32 = jnp.float32


def dot(a, b, ca, cb):
    return lax.dot_general(a, b, (((ca,), (cb,)), ((), ())), preferred_element_type=F32)


def kernel(
    q_hbm, k_hbm, v_hbm, g_hbm, gain_hbm, counts_hbm, flags_hbm,
    att_hbm, dq_hbm, dk_hbm, dv_hbm, gg_hbm,
    q_buf, g_buf, gain_ref, counts_ref, flags_ref, wide, rel_in, term_out, term_in, term_mid, total,
    part_in, cross_in, rel_total, probs_buf, low_buf, q_scaled, att_buf, dq_buf, gsum, gred, gg_ref,
    load_sem, swap_send, rel_recv, relay_send, kv_recv, fwd_send,
    term_send, term_recv, part_send, part_recv, cross_recv,
    fin_send, fin_recv, store_sem, gain_send, gain_recv,
):
    tower = lax.axis_index("tower")
    seq = lax.axis_index("seq")
    rep = lax.axis_index("rep")
    x_at, z_at, y_at = seq // 16, (seq // 4) % 4, seq % 4

    first = y_at == 0
    outer = first | (y_at == 3)
    inner = jnp.logical_not(outer)
    side = jnp.where(first, 3, 1)
    toward = jnp.where(first, BLOCKS - 1, 1)
    fwd_slot = jnp.where(first, 0, 2)
    cross_slot = 2 - fwd_slot
    cross_side = jnp.where(first, 0, 1)
    in_side = 1 - cross_side

    early_home = (first & (z_at == 0)) | ((y_at == 3) & (z_at == 3))
    early_relay = (first & (z_at == 3)) | ((y_at == 3) & (z_at == 0))
    home_shift = jnp.where(early_home, EARLY, 0)
    pass_shift = jnp.where(early_relay, LATE, 0)

    def shifted(block, step):
        return (block + step) % BLOCKS

    def along_z(block, step):
        return (block // 16) * 16 + ((block // 4 + step) % 4) * 4 + block % 4

    partner = (1 - tower, seq, rep)
    below = (tower, shifted(seq, BLOCKS - 1), rep)
    above = (tower, shifted(seq, 1), rep)
    my_relay = along_z(seq, side)
    relayed = along_z(seq, 4 - side)
    far_relay = (1 - tower, my_relay, rep)
    near_relay = (tower, my_relay, rep)
    relayed_home = (1 - tower, relayed, rep)
    relayed_query = (tower, relayed, rep)
    relayed_next = (tower, shifted(relayed, toward), rep)
    inside_next = (tower, shifted(seq, BLOCKS - toward), rep)
    term_relay = (tower, along_z(shifted(seq, toward), 4 - side), rep)

    group = (8, 4, 4)
    place = (y_at * 2 + rep, x_at, z_at)

    def along(axis, step):
        if axis == 0:
            spot = (place[0] + step) % 8
            return (tower, x_at * 16 + z_at * 4 + spot // 2, spot % 2)
        if axis == 1:
            return (tower, ((x_at + step) % 4) * 16 + z_at * 4 + y_at, rep)
        return (tower, along_z(seq, step), rep)

    loads = [
        pltpu.make_async_copy(q_hbm, q_buf, load_sem.at[0]),
        pltpu.make_async_copy(g_hbm, g_buf, load_sem.at[1]),
        pltpu.make_async_copy(gain_hbm, gain_ref, load_sem.at[2]),
        pltpu.make_async_copy(counts_hbm, counts_ref, load_sem.at[3]),
        pltpu.make_async_copy(flags_hbm, flags_ref, load_sem.at[4]),
    ]
    for copy in loads:
        copy.start()

    barrier = pltpu.get_barrier_semaphore()

    def greet(devices):
        for device in devices:
            pl.semaphore_signal(barrier, inc=1, device_id=device, device_id_type=MESH)
        pl.semaphore_wait(barrier, len(devices))

    everyone = []
    for axis in range(len(group)):
        everyone += [along(axis, step) for step in range(1, group[axis])]

    @pl.when(inner)
    def _():
        greet(everyone + [partner, below, above])

    @pl.when(outer)
    def _():
        greet(
            everyone
            + [inside_next, far_relay, near_relay, relayed_home]
            + [relayed_query, relayed_next, term_relay]
        )

    def columns(h):
        return pl.ds(h * DIM if isinstance(h, int) else pl.multiple_of(h * DIM, DIM), DIM)

    def remote(src, dst, send, recv, device):
        return pltpu.make_async_remote_copy(
            src_ref=src,
            dst_ref=dst,
            send_sem=send,
            recv_sem=recv,
            device_id=device,
            device_id_type=MESH,
        )

    sources = (k_hbm, v_hbm)
    targets = (dk_hbm, dv_hbm)

    def swap_copy(h, i):
        return remote(
            sources[i].at[:, columns(h)], wide.at[h, 1, i],
            swap_send.at[i], kv_recv.at[h, 1, i], partner,
        )

    def first_copy(h, i):
        return remote(
            sources[i].at[:, columns(h)], rel_in.at[h, i],
            swap_send.at[i], rel_recv.at[h, i], far_relay,
        )

    def relay_copies(h, i):
        return [
            remote(
                rel_in.at[h, i], wide.at[h, 1, i],
                relay_send.at[0], kv_recv.at[h, 1, i], relayed_query,
            ),
            remote(
                rel_in.at[h, i], wide.at[h, cross_slot, i],
                relay_send.at[1], kv_recv.at[h, cross_slot, i], relayed_next,
            ),
        ]

    def forward_both(h, i):
        return [
            remote(
                wide.at[h, 1, i], wide.at[h, j, i],
                fwd_send.at[j // 2], kv_recv.at[h, j, i], device,
            )
            for j, device in ((2, below), (0, above))
        ]

    def forward_inside(h, i):
        return [
            remote(
                wide.at[h, 1, i], wide.at[h, fwd_slot, i],
                fwd_send.at[0], kv_recv.at[h, fwd_slot, i], inside_next,
            )
        ]

    def terms_both(h, i):
        return [
            remote(
                term_out.at[h, j, i], term_in.at[h, j, i],
                term_send.at[j], term_recv.at[h, j, i], device,
            )
            for j, device in ((0, below), (1, above))
        ]

    def term_inside(h, i):
        return remote(
            term_out.at[h, in_side, i], term_in.at[h, in_side, i],
            term_send.at[0], term_recv.at[h, in_side, i], inside_next,
        )

    def term_cross(h, i):
        return remote(
            term_out.at[h, cross_side, i], cross_in.at[h, i],
            term_send.at[1], cross_recv.at[h, i], term_relay,
        )

    def term_arrival(h, i):
        return remote(
            term_out.at[h, 0, i], term_in.at[h, cross_side, i],
            term_send.at[0], term_recv.at[h, cross_side, i], inside_next,
        )

    def part_copy(h, i):
        return remote(
            total.at[h, i], part_in.at[h, i],
            part_send.at[0], part_recv.at[h, i], near_relay,
        )

    def final_copy(h, i, src, device):
        return remote(
            src.at[h, i], targets[i].at[:, columns(h)],
            fin_send.at[0], fin_recv.at[i], device,
        )

    def store_copies(h):
        return [
            pltpu.make_async_copy(att_buf.at[h], att_hbm.at[:, columns(h)], store_sem.at[0]),
            pltpu.make_async_copy(dq_buf.at[h], dq_hbm.at[:, columns(h)], store_sem.at[1]),
        ]

    def begin(copies):
        for copy in copies:
            copy.start()

    def arrived(copies):
        for copy in copies:
            copy.wait_recv()

    def sent(copies):
        for copy in copies:
            copy.wait_send()

    def either(relaying, direct):
        pl.when(outer)(relaying)
        pl.when(inner)(direct)

    def send_home(h, i):
        either(lambda: first_copy(h, i).start(), lambda: swap_copy(h, i).start())

    for part in range(AHEAD):
        send_home(part // 2, part % 2)

    @pl.when(early_home)
    def _():
        for part in range(AHEAD, AHEAD + 2 * EARLY):
            first_copy(part // 2, part % 2).start()

    for copy in loads:
        copy.wait()

    position = lax.broadcasted_iota(jnp.int32, (1, TOK), 1)
    bias = []
    for j in range(3):
        neighbour = seq + (j - 1)
        inside = jnp.clip(neighbour, 0, BLOCKS - 1)
        open_ = (neighbour == inside) & (flags_ref[j, tower, seq] == 1)
        live = jnp.where(open_, counts_ref[1 - tower, inside], 0)
        bias.append(jnp.where(position < live, 0.0, -1e30).astype(F32))
    bias = jnp.concatenate(bias, axis=1)
    gsum[...] = jnp.zeros_like(gsum)

    def relay(h, i):
        @pl.when(outer)
        def _():
            first_copy(h, i).wait_recv()
            begin(relay_copies(h, i))

    def forward(h, i):
        swap_copy(h, i).wait_recv()
        either(lambda: begin(forward_inside(h, i)), lambda: begin(forward_both(h, i)))

    def send_terms(h, i, left, right):
        terms = dot(left, right, 0, 0).astype(BF)
        term_out[h, 0, i] = terms[:TOK]
        term_mid[h, i] = terms[TOK : 2 * TOK]
        term_out[h, 1, i] = terms[2 * TOK :]
        either(
            lambda: begin([term_inside(h, i), term_cross(h, i)]),
            lambda: begin(terms_both(h, i)),
        )

    def compute(h, i):
        arrived(forward_both(h, i))
        gain = gain_ref[:, columns(h)]
        g = g_buf[:, columns(h)]
        if i == 0:
            q = (q_buf[:, columns(h)].astype(F32) * gain).astype(BF)
            q_scaled[...] = q
            keys = wide[h, :, 0].reshape(WIDE, DIM)
            scores = dot(q, keys, 1, 1) * SCALE + bias
            highest = jnp.max(scores, axis=1, keepdims=True)
            expo = jnp.exp(scores - highest)
            probs = expo / jnp.sum(expo, axis=1, keepdims=True)
            probs_buf[...] = probs
            low = probs.astype(BF)
            low_buf[...] = low
            send_terms(h, 1, low, g)
        else:
            keys = wide[h, :, 0].reshape(WIDE, DIM)
            values = wide[h, :, 1].reshape(WIDE, DIM)
            probs = probs_buf[...]
            dprob = dot(g, values, 1, 1)
            center = jnp.sum(probs * dprob, axis=1, keepdims=True)
            dscore = (probs * (dprob - center) * SCALE).astype(BF)
            send_terms(h, 0, dscore, q_scaled[...])
            att_buf[h] = dot(low_buf[...], values, 1, 0).astype(BF)
            dscaled = dot(dscore, keys, 1, 0)
            dq_buf[h] = (dscaled * gain).astype(BF)
            q_raw = q_buf[:, columns(h)].astype(F32)
            gsum[pl.ds(h, 1), :] = jnp.sum(q_raw * dscaled, axis=0, keepdims=True)
            begin(store_copies(h))

    def gather(h, part):
        i = 1 - part

        def relaying():
            term_arrival(h, i).wait_recv()
            total[h, i] = (
                term_mid[h, i].astype(F32) + term_in[h, cross_side, i].astype(F32)
            ).astype(BF)
            part_copy(h, i).start()

        def direct():
            arrived(terms_both(h, i))
            total[h, i] = (
                term_mid[h, i].astype(F32)
                + term_in[h, 0, i].astype(F32)
                + term_in[h, 1, i].astype(F32)
            ).astype(BF)
            final_copy(h, i, total, partner).start()

        either(relaying, direct)

    def pass_on(h, part):
        i = 1 - part

        @pl.when(outer)
        def _():
            part_copy(h, i).wait_recv()
            term_cross(h, i).wait_recv()
            rel_total[h, i] = (
                part_in[h, i].astype(F32) + cross_in[h, i].astype(F32)
            ).astype(BF)
            final_copy(h, i, rel_total, relayed_home).start()

    def relay_early(step, half):
        @pl.when(early_relay & (step < EARLY))
        def _():
            for i in range(2):
                relay(2 * step + half, i)

        @pl.when(early_relay & (step >= EARLY) & (step < HEADS - EARLY))
        def _():
            relay(step + EARLY, half)

    stages = (forward, compute, gather, pass_on)

    def advance(step, half):
        h = step + (half + AHEAD) // 2 + home_shift
        pl.when(h < HEADS)(functools.partial(send_home, h, (half + AHEAD) % 2))
        relay_early(step, half)
        pl.when(jnp.logical_not(early_relay) & (step < HEADS))(
            functools.partial(relay, step, half)
        )
        for stage, lag in zip((forward, compute), LAGS[1:3]):
            h = step + (half - lag) // 2
            pl.when((h >= 0) & (h < HEADS))(functools.partial(stage, h, (half - lag) % 2))
        for stage, lag, shift in ((gather, LAGS[3], 0), (pass_on, LAGS[4], pass_shift)):
            h = step + (half - lag) // 2 - shift
            pl.when((h >= 0) & (h < HEADS))(functools.partial(stage, h, (half - lag) % 2))

    def conclude(first_part):
        for part in range(first_part - LAGS[3], PARTS):
            gather(part // 2, part % 2)
        yield
        for part in range(first_part - LAGS[4] - 2 * LATE, PARTS):
            run = functools.partial(pass_on, part // 2, part % 2)
            if part < first_part - LAGS[4]:
                pl.when(early_relay)(run)
            else:
                run()
        yield

    looped = (PARTS + LAGS[2] + 1) // 2

    @pl.loop(0, looped)
    def _(step):
        advance(step, 0)
        advance(step, 1)

    def gain_copies(axis):
        return [
            remote(
                gred.at[axis, place[axis]], gred.at[axis, place[axis]],
                gain_send.at[axis, step], gain_recv.at[axis, step], along(axis, step),
            )
            for step in range(1, group[axis])
        ]

    def gain_arrivals(axis):
        return [
            remote(
                gred.at[axis, 0],
                gred.at[axis, (place[axis] + group[axis] - step) % group[axis]],
                gain_send.at[axis, step], gain_recv.at[axis, step], along(axis, step),
            )
            for step in range(1, group[axis])
        ]

    def gain_begin(axis, part):
        gred[axis, place[axis]] = part
        begin(gain_copies(axis))

    def gain_end(axis):
        arrived(gain_arrivals(axis))
        part = gred[axis, 0]
        for slot in range(1, group[axis]):
            part = part + gred[axis, slot]
        return part

    gain_begin(0, gsum[...])
    for axis, _ in enumerate(conclude(2 * looped)):
        gain_begin(axis + 1, gain_end(axis))

    def all_sent(ref, sems):
        for sem in sems:
            remote(ref, ref, sem, sem, partner).wait_send()

    all_sent(k_hbm, [swap_send.at[0], swap_send.at[1]])
    all_sent(total, [fwd_send.at[0], term_send.at[0], term_send.at[1], fin_send.at[0]])

    @pl.when(outer)
    def _():
        all_sent(total, [relay_send.at[0], relay_send.at[1], part_send.at[0]])

    @pl.when(inner)
    def _():
        all_sent(total, [fwd_send.at[1]])

    for i in range(2):
        pltpu.make_async_copy(att_buf, dq_buf, store_sem.at[i]).wait()

    part = gain_end(2)
    for h in range(HEADS):
        gg_ref[:, h * DIM : (h + 1) * DIM] = part[h : h + 1]
    gg_copy = pltpu.make_async_copy(gg_ref, gg_hbm, load_sem.at[5])
    gg_copy.start()
    for axis in range(len(group)):
        sent(gain_copies(axis))

    for i in range(2):
        remote(k_hbm, targets[i], fin_send.at[0], fin_recv.at[i], partner).wait_recv()

    gg_copy.wait()


def keep(*refs):
    copies = []
    for i in range(4):
        for half in range(4):
            rows = pl.ds(half * 64, 64)
            held = refs[10].at[i, rows]
            copies.append(
                (
                    pltpu.make_async_copy(refs[i].at[rows], held, refs[11].at[0, i, half]),
                    pltpu.make_async_copy(held, refs[i + 5].at[rows], refs[11].at[1, i, half]),
                )
            )
    copies.append(
        (
            pltpu.make_async_copy(refs[4], refs[12], refs[13].at[0]),
            pltpu.make_async_copy(refs[12], refs[9], refs[13].at[1]),
        )
    )
    for load, _ in copies:
        load.start()
    for load, store in copies:
        load.wait()
        store.start()
    for _, store in copies:
        store.wait()


def per_device(query_rows, key_rows, value_rows, out_grad, query_gain, live_counts, intersection):
    anywhere = pl.BlockSpec(memory_space=pl.ANY)
    block = jax.ShapeDtypeStruct((TOK, WIDTH), BF)
    dma = pltpu.SemaphoreType.DMA
    pair = (HEADS, 2)
    quad = (HEADS, 2, 2)
    shapes = (block, block, block, block, jax.ShapeDtypeStruct((1, WIDTH), F32))
    results = pl.pallas_call(
        kernel,
        out_shape=shapes,
        in_specs=[anywhere] * 7,
        out_specs=(anywhere,) * 5,
        scratch_shapes=[
            pltpu.VMEM((TOK, WIDTH), BF),
            pltpu.VMEM((TOK, WIDTH), BF),
            pltpu.VMEM((1, WIDTH), F32),
            pltpu.SMEM((2, BLOCKS), jnp.int32),
            pltpu.SMEM((3, 2, BLOCKS), jnp.int32),
            pltpu.VMEM((HEADS, 3, 2, TOK, DIM), BF),
            pltpu.VMEM((HEADS, 2, TOK, DIM), BF),
            pltpu.VMEM((HEADS, 2, 2, TOK, DIM), BF),
            pltpu.VMEM((HEADS, 2, 2, TOK, DIM), BF),
            pltpu.VMEM((HEADS, 2, TOK, DIM), BF),
            pltpu.VMEM((HEADS, 2, TOK, DIM), BF),
            pltpu.VMEM((HEADS, 2, TOK, DIM), BF),
            pltpu.VMEM((HEADS, 2, TOK, DIM), BF),
            pltpu.VMEM((HEADS, 2, TOK, DIM), BF),
            pltpu.VMEM((TOK, WIDE), F32),
            pltpu.VMEM((TOK, WIDE), BF),
            pltpu.VMEM((TOK, DIM), BF),
            pltpu.VMEM((HEADS, TOK, DIM), BF),
            pltpu.VMEM((HEADS, TOK, DIM), BF),
            pltpu.VMEM((16, DIM), F32),
            pltpu.VMEM((3, 8, 16, DIM), F32),
            pltpu.VMEM((1, WIDTH), F32),
            dma((6,)), dma((2,)), dma(pair), dma((2,)), dma((HEADS, 3, 2)), dma((2,)),
            dma((2,)), dma(quad), dma((1,)), dma(pair), dma(pair),
            dma((1,)), dma((2,)), dma((2,)), dma((3, 8)), dma((3, 8)),
        ],
        compiler_params=pltpu.CompilerParams(
            collective_id=0, has_side_effects=True, vmem_limit_bytes=VMEM_MIB * 2**20
        ),
        name="cross_attention",
    )(
        query_rows[0, 0], key_rows[0, 0], value_rows[0, 0], out_grad[0, 0],
        query_gain, live_counts, jnp.transpose(intersection, (2, 0, 1)),
    )
    results = pl.pallas_call(
        keep,
        out_shape=shapes,
        in_specs=[anywhere] * 5,
        out_specs=(anywhere,) * 5,
        scratch_shapes=[
            pltpu.VMEM((4, TOK, WIDTH), BF), dma((2, 4, 4)),
            pltpu.VMEM((1, WIDTH), F32), dma((2,)),
        ],
        compiler_params=pltpu.CompilerParams(vmem_limit_bytes=VMEM_MIB * 2**20),
        name="keep",
    )(*results)
    shape = (1, 1, TOK, WIDTH)
    return tuple(r.reshape(shape) for r in results[:4]) + (results[4],)


def solution(mesh):
    rows = P("tower", "rep", "seq", None)
    return jax.shard_map(
        per_device,
        mesh=mesh,
        in_specs=(rows, rows, rows, rows, P("tower", None), P(), P()),
        out_specs=(rows, rows, rows, rows, P("tower", None)),
        check_vma=False,
    )
```
